256 devices in a mesh: items: 32 (over x, y, core), codes: 8 (over z).
Axes of the slice: x: 4, y: 4, z: 8, core: 2. Of those that a mesh axis runs over, the one named last changes fastest.
Arguments:
- residuals: bfloat16 [65536, 256], P('items', 'codes'), may hold values from -6 to 6
- codebook: bfloat16 [8192, 256], P('codes'), may hold values from -6 to 6
Outputs:
- soft_codes: float32 [65536, 256], P('items', 'codes')
- items_scale: float32 [65536], P('items')
- code_weights: float32 [8192], P('codes')
The draws below stay inside these ranges and needn't reach their ends.
All inputs are finite; a program needn't handle non-finite values.
Results may differ from the reference program's by a relative error of at most 0.0014.
Values may be sent and summed in bfloat16 or wider, within the bound.
A program may use at most 64 MiB of HBM per device.

```python
import jax
import jax.numpy as jnp
from jax import lax

F = 256
CODES = 8192
ITERS = 3
ITEMS = 65536


def shard_levels(stream_key, dims, shards, low, top_value):
    level, own = 1.0, jax.random.fold_in(stream_key, 6)
    for axis_at, shards_of in shards:
        steps = jnp.exp(jax.random.uniform(jax.random.fold_in(own, axis_at), (shards_of,), jnp.float32, low / len(shards), top_value / len(shards)))
        level = level * jnp.repeat(steps, dims[axis_at] // shards_of).reshape([-1 if axis == axis_at else 1 for axis in range(len(dims))])
    return level


def gaussian(key, dims, spread, reach, shards=(), held_as=jnp.bfloat16):
    drawn = spread * jax.random.normal(key, dims, jnp.float32)
    if shards:
        drawn = drawn * shard_levels(key, dims, shards, -0.22, 0.18)
    return jnp.clip(drawn, -reach, reach).astype(held_as)


def setup_inputs(seed: int = 0) -> dict:
    seeds = jax.random.split(jax.random.key(seed), 3)
    return {
        "residuals": gaussian(seeds[0], (ITEMS, F), 1.0, 6.0, ((0, 32), (1, 8))),
        "codebook": gaussian(seeds[1], (CODES, F), 1.0, 6.0, ((0, 8),)),
    }


eps_value = 1e-06
entropic_smoothing = 32.0
affinity_shift = 2.0

def inverse_scale(values):
    wide = values.astype(jnp.float32)
    return lax.rsqrt(lax.optimization_barrier(jnp.mean(wide * wide, axis=-1)) + eps_value)

def kernel_tile(rows, row_inv, codes, reciprocal_centroid_factor):
    dots = jnp.dot(rows, codes.T, preferred_element_type=jnp.float32)
    angular_affinity = dots * row_inv[:, None] * reciprocal_centroid_factor[None, :] / F
    return jnp.exp(entropic_smoothing * angular_affinity - affinity_shift)

def reference(residuals, codebook):
    block = min(1024, ITEMS)
    count = ITEMS // block
    row_blocks = residuals.reshape(count, block, F)
    row_scales = inverse_scale(residuals).reshape(count, block)
    reciprocal_centroid_factor = inverse_scale(codebook)
    items_scale = jnp.ones((ITEMS,), jnp.float32)
    code_weights = jnp.ones((CODES,), jnp.float32)
    for iteration in range(ITERS):

        def column_step(total, item):
            rows, scales, weights = item
            tile = kernel_tile(rows, scales, codebook, reciprocal_centroid_factor)
            return (total + lax.optimization_barrier(jnp.sum(tile * weights[:, None], axis=0)), None)
        totals, discarded_output = lax.scan(column_step, jnp.zeros((CODES,), jnp.float32), (row_blocks, row_scales, items_scale.reshape(count, block)))
        code_weights = ITEMS / totals

        def left_factor_update(item):
            rows, scales = item
            tile = kernel_tile(rows, scales, codebook, reciprocal_centroid_factor)
            return lax.optimization_barrier(jnp.sum(tile * code_weights[None, :], axis=1))
        items_scale = (CODES / lax.map(left_factor_update, (row_blocks, row_scales))).reshape(ITEMS)

    def soft_step(item):
        rows, scales = item
        tile = kernel_tile(rows, scales, codebook, reciprocal_centroid_factor)
        assignment_shares = (tile * (code_weights / CODES)[None, :]).astype(jnp.bfloat16)
        return jnp.dot(assignment_shares, codebook, preferred_element_type=jnp.float32)
    mixture = lax.map(soft_step, (row_blocks, row_scales)).reshape(ITEMS, F)
    soft_codes = items_scale[:, None] * mixture
    return (soft_codes, items_scale, code_weights)
```

```python
import functools

import jax
import jax.numpy as jnp
from jax import lax
from jax.experimental import pallas as pl
from jax.experimental.pallas import tpu as pltpu
from jax.sharding import PartitionSpec as P

F = 256
ITERS = 3
EPS = 1e-06
SMOOTHING = 32.0
SHIFT = 2.0
LOG2E = 1.4426950408889634

LANES = 128
CHUNK = 512
TILE = 128
MESH = pl.DeviceIdType.MESH


def kernel(
    items_n, codes_n, total_items, total_codes,
    rt_hbm, cb_hbm, parts_ref, s_ref, w_ref,
    cb, R, K, inv_row, inv_col, tacc, W, tsend, colbuf, rowbuf,
    in_sem, ring_send, ring_recv, col_send, col_recv, row_send, row_recv,
):
    me_i = lax.axis_index("items")
    me_z = lax.axis_index("codes")
    rows = rt_hbm.shape[1]
    codes = cb_hbm.shape[0]
    feats = rt_hbm.shape[0]
    chunks = rows // CHUNK
    right = lax.rem(me_z + 1, codes_n)
    left = lax.rem(me_z + codes_n - 1, codes_n)
    half = codes_n // 2

    def block(c, z):
        return R.at[c, pl.ds(pl.multiple_of(z * feats, feats), feats), :]

    own = [
        pltpu.make_async_copy(
            rt_hbm.at[:, c * CHUNK:(c + 1) * CHUNK], block(c, me_z), in_sem.at[c]
        )
        for c in range(chunks)
    ]
    for copy in own:
        copy.start()
    load_cb = pltpu.make_async_copy(cb_hbm, cb, in_sem.at[chunks])
    load_cb.start()

    barrier = pltpu.get_barrier_semaphore()

    def greet_items(k, carry):
        pl.semaphore_signal(
            barrier, inc=1, device_id={"items": lax.rem(me_i + k, items_n)}, device_id_type=MESH
        )
        return carry

    def greet_codes(k, carry):
        pl.semaphore_signal(
            barrier, inc=1, device_id={"codes": lax.rem(me_z + k, codes_n)}, device_id_type=MESH
        )
        return carry

    lax.fori_loop(1, codes_n, greet_codes, 0)
    lax.fori_loop(1, items_n, greet_items, 0)
    pl.semaphore_wait(barrier, items_n + codes_n - 2)

    def hop(direction, h, c):
        z = me_z - (h - 1) if direction == 0 else me_z + (h - 1)
        z = lax.rem(z + codes_n, codes_n)
        ref = block(c, z)
        return pltpu.make_async_remote_copy(
            src_ref=ref, dst_ref=ref,
            send_sem=ring_send.at[direction, h - 1, c],
            recv_sem=ring_recv.at[direction, h - 1, c],
            device_id={"codes": right if direction == 0 else left},
            device_id_type=MESH,
        )

    def goes(direction, h, c):
        return h < half or (h == half and (c < chunks // 2) == (direction == 0))

    for c in range(chunks):
        own[c].wait()
        for d in range(2):
            if goes(d, 1, c):
                hop(d, 1, c).start()
    load_cb.wait()

    wide = cb[...].astype(jnp.float32)
    inv_col[...] = jnp.broadcast_to(
        lax.rsqrt(jnp.mean(wide * wide, axis=1, keepdims=True) + EPS), inv_col.shape
    )
    tacc[...] = jnp.zeros_like(tacc)

    for h in range(1, half + 1):
        for c in range(chunks):
            for d in range(2):
                if goes(d, h, c):
                    hop(d, h, c).wait_recv()
                    if goes(d, h + 1, c):
                        hop(d, h + 1, c).start()

    for c in range(chunks):
        r_wide = R[c].astype(jnp.float32)
        inv_row[...] = lax.rsqrt(
            jnp.mean(r_wide * r_wide, axis=0, keepdims=True) + EPS
        ) * (SMOOTHING * LOG2E / F)

        def tile_step(m, carry, c=c):
            at = pl.ds(pl.multiple_of(m * TILE, TILE), TILE)
            dots = jnp.dot(cb[at, :], R[c], preferred_element_type=jnp.float32)
            scale = inv_col[at, :]
            total = tacc[at, :]
            for q in range(CHUNK // LANES):
                lanes = slice(q * LANES, (q + 1) * LANES)
                value = jnp.exp2(dots[:, lanes] * inv_row[:, lanes] * scale - SHIFT * LOG2E)
                K[at, c * CHUNK + q * LANES:c * CHUNK + (q + 1) * LANES] = value
                total = total + value
            tacc[at, :] = total
            return carry

        lax.fori_loop(0, codes // TILE, tile_step, 0)

    groups = codes // 8
    lane_chunks = rows // LANES

    def exchange(buf, it, mine, count, axis, send_sem, recv_sem):
        def send(k, carry):
            pltpu.make_async_remote_copy(
                src_ref=buf.at[it, mine], dst_ref=buf.at[it, mine],
                send_sem=send_sem.at[it], recv_sem=recv_sem.at[it],
                device_id={axis: lax.rem(mine + k, count)}, device_id_type=MESH,
            ).start()
            return carry

        lax.fori_loop(1, count, send, 0)

    def all_but_one(buf, it, count, sem):
        ref = buf.at[it, pl.ds(0, count - 1)]
        return pltpu.make_async_copy(ref, ref, sem.at[it])

    for it in range(ITERS):
        if it > 0:
            s_bcast = [
                jnp.broadcast_to(s_ref[q:q + 1, :], (8, LANES)) for q in range(lane_chunks)
            ]

            def col_step(g, carry):
                at = pl.ds(pl.multiple_of(g * 8, 8), 8)
                total = K[at, 0:LANES] * s_bcast[0]
                for q in range(1, lane_chunks):
                    total = total + K[at, q * LANES:(q + 1) * LANES] * s_bcast[q]
                tacc[at, :] = total
                return carry

            lax.fori_loop(0, groups, col_step, 0, unroll=4)
        for b in range(codes // LANES):
            blockT = jnp.transpose(tacc[b * LANES:(b + 1) * LANES, :])
            tsend[b:b + 1, :] = jnp.sum(blockT, axis=0, keepdims=True)
        colbuf[it, me_i] = tsend[...]
        exchange(colbuf, it, me_i, items_n, "items", col_send, col_recv)
        all_but_one(colbuf, it, items_n, col_recv).wait()
        w = total_items / jnp.sum(colbuf[it], axis=0)
        w_ref[...] = w
        for b in range(codes // LANES):
            W[b * LANES:(b + 1) * LANES, :] = jnp.transpose(
                jnp.broadcast_to(w[b:b + 1, :], (LANES, LANES))
            )

        def row_step(g, acc):
            at = pl.ds(pl.multiple_of(g * 8, 8), 8)
            weight = W[at, :]
            return tuple(
                acc[q] + K[at, q * LANES:(q + 1) * LANES] * weight for q in range(lane_chunks)
            )

        acc = lax.fori_loop(
            0, groups, row_step,
            tuple(jnp.zeros((8, LANES), jnp.float32) for _ in range(lane_chunks)), unroll=4,
        )
        for q in range(lane_chunks):
            s_ref[q:q + 1, :] = jnp.sum(acc[q], axis=0, keepdims=True)
        rowbuf[it, me_z] = s_ref[...]
        exchange(rowbuf, it, me_z, codes_n, "codes", row_send, row_recv)
        if it == ITERS - 1:
            def soft_step(n, carry):
                lanes = pl.ds(pl.multiple_of(n * 256, 256), 256)
                weight = W[...] * (1.0 / total_codes)
                shares = (K[:, lanes] * jnp.concatenate([weight, weight], axis=1)).astype(jnp.bfloat16)
                parts_ref[:, lanes] = lax.dot_general(
                    cb[...], shares, (((0,), (0,)), ((), ())), preferred_element_type=jnp.float32
                )
                return carry

            lax.fori_loop(0, rows // 256, soft_step, 0)
        all_but_one(rowbuf, it, codes_n, row_recv).wait()
        s_ref[...] = total_codes / jnp.sum(rowbuf[it], axis=0)

    for it in range(ITERS):
        all_but_one(colbuf, it, items_n, col_send).wait()
        all_but_one(rowbuf, it, codes_n, row_send).wait()
    for h in range(1, half + 1):
        for c in range(chunks):
            for d in range(2):
                if goes(d, h, c):
                    hop(d, h, c).wait_send()


def shards(residuals, codebook):
    items_n, codes_n = lax.axis_size("items"), lax.axis_size("codes")
    rows, feats = residuals.shape
    codes = codebook.shape[0]
    chunks = rows // CHUNK
    half = codes_n // 2
    f32 = jnp.float32
    any_space = pl.BlockSpec(memory_space=pl.ANY)
    vmem = pl.BlockSpec(memory_space=pltpu.VMEM)
    parts, items_scale, code_weights = pl.pallas_call(
        functools.partial(
            kernel, items_n, codes_n, float(rows * items_n), float(codes * codes_n)
        ),
        out_shape=(
            jax.ShapeDtypeStruct((F, rows), f32),
            jax.ShapeDtypeStruct((rows // LANES, LANES), f32),
            jax.ShapeDtypeStruct((codes // LANES, LANES), f32),
        ),
        in_specs=[any_space, any_space],
        out_specs=(vmem, vmem, vmem),
        scratch_shapes=[
            pltpu.VMEM((codes, F), jnp.bfloat16),
            pltpu.VMEM((chunks, F, CHUNK), jnp.bfloat16),
            pltpu.VMEM((codes, rows), f32),
            pltpu.VMEM((1, CHUNK), f32),
            pltpu.VMEM((codes, LANES), f32),
            pltpu.VMEM((codes, LANES), f32),
            pltpu.VMEM((codes, LANES), f32),
            pltpu.VMEM((codes // LANES, LANES), f32),
            pltpu.VMEM((ITERS, items_n, codes // LANES, LANES), f32),
            pltpu.VMEM((ITERS, codes_n, rows // LANES, LANES), f32),
            pltpu.SemaphoreType.DMA((chunks + 1,)),
            pltpu.SemaphoreType.DMA((2, half, chunks)),
            pltpu.SemaphoreType.DMA((2, half, chunks)),
            pltpu.SemaphoreType.DMA((ITERS,)),
            pltpu.SemaphoreType.DMA((ITERS,)),
            pltpu.SemaphoreType.DMA((ITERS,)),
            pltpu.SemaphoreType.DMA((ITERS,)),
        ],
        compiler_params=pltpu.CompilerParams(
            collective_id=0, has_side_effects=True, vmem_limit_bytes=48 * 1024 * 1024
        ),
    )(residuals.T, codebook)
    items_scale = items_scale.reshape(rows)
    mixture = lax.psum_scatter(parts, "codes", scatter_dimension=0, tiled=True)
    soft_codes = (mixture * items_scale[None, :]).T
    return soft_codes, items_scale, code_weights.reshape(codes)


def solution(mesh):
    placed = (P("items", "codes"), P("codes", None))
    return jax.shard_map(
        shards,
        mesh=mesh,
        in_specs=placed,
        out_specs=(P("items", "codes"), P("items"), P("codes")),
        check_vma=False,
    )
```

```python
import functools

import jax
import jax.numpy as jnp
from jax import lax
from jax.experimental import pallas as pl
from jax.experimental.pallas import tpu as pltpu
from jax.sharding import PartitionSpec as P

F = 256
ITERS = 3
EPS = 1e-06
SMOOTHING = 32.0
SHIFT = 2.0
LOG2E = 1.4426950408889634

LANES = 128
CHUNK = 512
TILE = 128
SIDE = 4
MESH = pl.DeviceIdType.MESH


def kernel(
    items_n, codes_n, total_items, total_codes,
    rt_hbm, cb_hbm, soft_ref, s_ref, w_ref,
    cb, cbf, R, K, K2, inv_row, inv_col, tacc, W, tsend, cinv, wbuf, colbuf, rowbuf, sbuf,
    a2, mix, shares, softT, land,
    in_sem, ring_send, ring_recv, col_send, col_recv, row_send, row_recv,
    z_send, z_recv, plane_send, plane_recv, pair_send, pair_recv, out_send, out_recv,
):
    me_i = lax.axis_index("items")
    me_z = lax.axis_index("codes")
    x, y, core = me_i // (2 * SIDE), lax.rem(me_i // 2, SIDE), lax.rem(me_i, 2)
    rows = rt_hbm.shape[1]
    codes = cb_hbm.shape[0]
    feats = rt_hbm.shape[0]
    chunks = rows // CHUNK
    mine = rows // codes_n
    right = lax.rem(me_z + 1, codes_n)
    left = lax.rem(me_z + codes_n - 1, codes_n)
    half = codes_n // 2

    def remote(src, dst, send, recv, device):
        return pltpu.make_async_remote_copy(
            src_ref=src, dst_ref=dst, send_sem=send, recv_sem=recv,
            device_id=device, device_id_type=MESH,
        )

    def wait_bytes(ref, sem):
        pltpu.make_async_copy(ref, ref, sem).wait()

    def at_plane(px, py, pcore):
        return {"items": (px * SIDE + py) * 2 + pcore}

    def block(c, z):
        return R.at[c, pl.ds(pl.multiple_of(z * feats, feats), feats), :]

    own = [
        pltpu.make_async_copy(
            rt_hbm.at[:, c * CHUNK:(c + 1) * CHUNK], block(c, me_z), in_sem.at[c]
        )
        for c in range(chunks)
    ]
    for copy in own:
        copy.start()
    load_cb = pltpu.make_async_copy(cb_hbm, cb, in_sem.at[chunks])
    load_cb.start()

    barrier = pltpu.get_barrier_semaphore()

    def greet_items(k, carry):
        pl.semaphore_signal(
            barrier, inc=1, device_id={"items": lax.rem(me_i + k, items_n)}, device_id_type=MESH
        )
        return carry

    def greet_codes(k, carry):
        pl.semaphore_signal(
            barrier, inc=1, device_id={"codes": lax.rem(me_z + k, codes_n)}, device_id_type=MESH
        )
        return carry

    lax.fori_loop(1, codes_n, greet_codes, 0)
    lax.fori_loop(1, items_n, greet_items, 0)

    load_cb.wait()
    wide = cb[...].astype(jnp.float32)
    inv_col[...] = jnp.broadcast_to(
        lax.rsqrt(jnp.mean(wide * wide, axis=1, keepdims=True) + EPS), inv_col.shape
    )
    for b in range(codes // LANES):
        tsend[b:b + 1, :] = jnp.transpose(inv_col[b * LANES:(b + 1) * LANES, :])[0:1, :]
    cinv[me_z] = tsend[...]
    cbf[me_z, x, y, core] = cb[pl.ds(pl.multiple_of(me_i * 32, 32), 32), :].reshape(2, 16, F)

    pl.semaphore_wait(barrier, items_n + codes_n - 2)

    def hop(direction, h, c):
        z = me_z - (h - 1) if direction == 0 else me_z + (h - 1)
        ref = block(c, lax.rem(z + codes_n, codes_n))
        return remote(
            ref, ref, ring_send.at[direction, h - 1, c], ring_recv.at[direction, h - 1, c],
            {"codes": right if direction == 0 else left},
        )

    def goes(direction, h, c):
        return h < half or (h == half and (c < chunks // 2) == (direction == 0))

    for c in range(chunks):
        own[c].wait()
        for d in range(2):
            if goes(d, 1, c):
                hop(d, 1, c).start()

    def send_codes(k, carry):
        to = {"codes": lax.rem(me_z + k, codes_n)}
        piece = cbf.at[me_z, x, y, core]
        remote(piece, piece, z_send.at[0], z_recv.at[0], to).start()
        remote(cinv.at[me_z], cinv.at[me_z], z_send.at[1], z_recv.at[1], to).start()
        return carry

    lax.fori_loop(1, codes_n, send_codes, 0)

    def plane_copies(stage):
        if stage == 0:
            a, b = cbf.at[:, x, y, core, 0], cbf.at[:, x, y, core, 1]
        else:
            b, a = cbf.at[:, :, y, core, 0], cbf.at[:, x, :, core, 1]
        out = []
        for k in range(1, SIDE):
            to_x = at_plane(lax.rem(x + k, SIDE), y, core)
            to_y = at_plane(x, lax.rem(y + k, SIDE), core)
            out.append(remote(a, a, plane_send.at[stage, 0], plane_recv.at[stage, 0], to_x))
            out.append(remote(b, b, plane_send.at[stage, 1], plane_recv.at[stage, 1], to_y))
        return out

    def plane_wait(stage, sem):
        for way in range(2):
            if stage == 0:
                ref = cbf.at[:, 0, pl.ds(0, SIDE - 1), 0, 0]
            else:
                ref = cbf.at[:, :, pl.ds(0, SIDE - 1), 0, 0]
            wait_bytes(ref, sem.at[stage, way])

    def pair_copy():
        ref = cbf.at[:, :, :, core]
        return remote(ref, ref, pair_send, pair_recv, at_plane(x, y, 1 - core))

    for h in range(1, half + 1):
        for c in range(chunks):
            for d in range(2):
                if goes(d, h, c):
                    hop(d, h, c).wait_recv()
                    if goes(d, h + 1, c):
                        hop(d, h + 1, c).start()
        if h == 2:
            wait_bytes(cbf.at[pl.ds(0, codes_n - 1), 0, 0, 0], z_recv.at[0])
            wait_bytes(cinv.at[pl.ds(0, codes_n - 1)], z_recv.at[1])
            for copy in plane_copies(0):
                copy.start()

    plane_wait(0, plane_recv)
    for copy in plane_copies(1):
        copy.start()

    tacc[...] = jnp.zeros_like(tacc)
    for c in range(chunks):
        r_wide = R[c].astype(jnp.float32)
        inv_row[...] = lax.rsqrt(
            jnp.mean(r_wide * r_wide, axis=0, keepdims=True) + EPS
        ) * (SMOOTHING * LOG2E / F)

        def tile_step(m, carry, c=c):
            at = pl.ds(pl.multiple_of(m * TILE, TILE), TILE)
            dots = jnp.dot(cb[at, :], R[c], preferred_element_type=jnp.float32)
            scale = inv_col[at, :]
            total = tacc[at, :]
            for q in range(CHUNK // LANES):
                lanes = slice(q * LANES, (q + 1) * LANES)
                value = jnp.exp2(dots[:, lanes] * inv_row[:, lanes] * scale - SHIFT * LOG2E)
                K[at, c * CHUNK + q * LANES:c * CHUNK + (q + 1) * LANES] = value
                total = total + value
            tacc[at, :] = total
            return carry

        lax.fori_loop(0, codes // TILE, tile_step, 0)

    groups = codes // 8
    lane_chunks = rows // LANES

    def exchange(buf, mine_at, count, axis, send_sem, recv_sem):
        def send(k, carry):
            ref = buf.at[mine_at]
            remote(ref, ref, send_sem, recv_sem, {axis: lax.rem(mine_at + k, count)}).start()
            return carry

        lax.fori_loop(1, count, send, 0)

    def all_but_one(buf, count, sem):
        wait_bytes(buf.at[pl.ds(0, count - 1)], sem)

    def second_tile():
        my_rows = R[me_z // (CHUNK // mine), :, pl.ds(
            pl.multiple_of(lax.rem(me_z, CHUNK // mine) * mine, mine), mine)]
        rows2 = jnp.transpose(my_rows)
        wide2 = rows2.astype(jnp.float32)
        a2[...] = jnp.broadcast_to(
            lax.rsqrt(jnp.mean(wide2 * wide2, axis=1, keepdims=True) + EPS)
            * (SMOOTHING * LOG2E / F), a2.shape)
        softT[...] = wide2

        def step(n, carry):
            z, k = n // 4, lax.rem(n, 4)
            some = cbf[z, k].reshape(codes // 4, F)
            dots = lax.dot_general(
                softT[...].astype(jnp.bfloat16), some, (((1,), (1,)), ((), ())),
                preferred_element_type=jnp.float32,
            )
            for q in range(2):
                scale = cinv[z, pl.ds(2 * k + q, 1), :]
                value = jnp.exp2(
                    dots[:, q * LANES:(q + 1) * LANES] * a2[...] * scale - SHIFT * LOG2E)
                K2[:, pl.ds(pl.multiple_of(n * 256 + q * LANES, LANES), LANES)] = value
            return carry

        lax.fori_loop(0, codes_n * 4, step, 0)

    for it in range(ITERS):
        last = it == ITERS - 1
        if it > 0:
            s_bcast = [
                jnp.broadcast_to(s_ref[q:q + 1, :], (8, LANES)) for q in range(lane_chunks)
            ]

            def col_step(g, carry):
                at = pl.ds(pl.multiple_of(g * 8, 8), 8)
                total = K[at, 0:LANES] * s_bcast[0]
                for q in range(1, lane_chunks):
                    total = total + K[at, q * LANES:(q + 1) * LANES] * s_bcast[q]
                tacc[at, :] = total
                return carry

            lax.fori_loop(0, groups, col_step, 0, unroll=4)
        for b in range(codes // LANES):
            blockT = jnp.transpose(tacc[b * LANES:(b + 1) * LANES, :])
            tsend[b:b + 1, :] = jnp.sum(blockT, axis=0, keepdims=True)
        colbuf[it, me_i] = tsend[...]
        exchange(colbuf.at[it], me_i, items_n, "items", col_send.at[it], col_recv.at[it])
        if it == 1:
            plane_wait(1, plane_recv)
            pair_copy().start()
        if last:
            pair_copy().wait_recv()
            second_tile()
        all_but_one(colbuf.at[it], items_n, col_recv.at[it])
        w = total_items / jnp.sum(colbuf[it], axis=0)
        if last:
            w_ref[...] = w
            wbuf[me_z] = w * (1.0 / total_codes)
            exchange(wbuf, me_z, codes_n, "codes", row_send.at[it], row_recv.at[it])
            all_but_one(wbuf, codes_n, row_recv.at[it])
            break
        for b in range(codes // LANES):
            W[b * LANES:(b + 1) * LANES, :] = jnp.transpose(
                jnp.broadcast_to(w[b:b + 1, :], (LANES, LANES))
            )

        def row_step(g, acc):
            at = pl.ds(pl.multiple_of(g * 8, 8), 8)
            weight = W[at, :]
            return tuple(
                acc[q] + K[at, q * LANES:(q + 1) * LANES] * weight for q in range(lane_chunks)
            )

        acc = lax.fori_loop(
            0, groups, row_step,
            tuple(jnp.zeros((8, LANES), jnp.float32) for _ in range(lane_chunks)), unroll=4,
        )
        for q in range(lane_chunks):
            s_ref[q:q + 1, :] = jnp.sum(acc[q], axis=0, keepdims=True)
        rowbuf[it, me_z] = s_ref[...]
        exchange(rowbuf.at[it], me_z, codes_n, "codes", row_send.at[it], row_recv.at[it])
        all_but_one(rowbuf.at[it], codes_n, row_recv.at[it])
        s_ref[...] = total_codes / jnp.sum(rowbuf[it], axis=0)

    mix[...] = jnp.zeros_like(mix)
    a2[...] = jnp.zeros_like(a2)

    def soft_step(z, carry):
        total = a2[...]
        for q in range(codes // LANES):
            value = K2[:, pl.ds(pl.multiple_of(z * codes + q * LANES, LANES), LANES)]
            value = value * wbuf[z, pl.ds(q, 1), :]
            total = total + value
            shares[:, q * LANES:(q + 1) * LANES] = value.astype(jnp.bfloat16)
        a2[...] = total
        mix[...] += jnp.dot(
            shares[...], cbf[z].reshape(codes, F), preferred_element_type=jnp.float32
        )
        return carry

    lax.fori_loop(0, codes_n, soft_step, 0)
    for b in range(mine // LANES):
        at = slice(b * LANES, (b + 1) * LANES)
        scale = 1.0 / jnp.sum(jnp.transpose(a2[at, :]), axis=0, keepdims=True)
        sbuf[me_z, b:b + 1, :] = scale
        softT[:, at] = jnp.transpose(mix[at, :]) * scale

    def part(z):
        return pl.ds(pl.multiple_of(z * feats, feats), feats)

    my_lanes = pl.ds(pl.multiple_of(me_z * mine, mine), mine)

    def send_out(k, carry):
        z = lax.rem(me_z + k, codes_n)
        remote(softT.at[part(z), :], land.at[:, my_lanes], out_send.at[0], out_recv.at[0],
               {"codes": z}).start()
        remote(sbuf.at[me_z], sbuf.at[me_z], out_send.at[1], out_recv.at[1],
               {"codes": z}).start()
        return carry

    lax.fori_loop(1, codes_n, send_out, 0)
    land[:, my_lanes] = softT[part(me_z), :]
    sent = land.at[:, pl.ds(0, (codes_n - 1) * mine)]
    some = sbuf.at[pl.ds(0, codes_n - 1)]
    wait_bytes(sent, out_recv.at[0])
    wait_bytes(some, out_recv.at[1])
    soft_ref[...] = land[...]
    for z in range(codes_n):
        for b in range(mine // LANES):
            n = z * (mine // LANES) + b
            s_ref[n:n + 1, :] = sbuf[z, b:b + 1, :]

    wait_bytes(sent, out_send.at[0])
    wait_bytes(some, out_send.at[1])
    for it in range(ITERS):
        all_but_one(colbuf.at[it], items_n, col_send.at[it])
        if it < ITERS - 1:
            all_but_one(rowbuf.at[it], codes_n, row_send.at[it])
        else:
            all_but_one(wbuf, codes_n, row_send.at[it])
    wait_bytes(cbf.at[pl.ds(0, codes_n - 1), 0, 0, 0], z_send.at[0])
    wait_bytes(cinv.at[pl.ds(0, codes_n - 1)], z_send.at[1])
    plane_wait(0, plane_send)
    plane_wait(1, plane_send)
    pair_copy().wait_send()
    for h in range(1, half + 1):
        for c in range(chunks):
            for d in range(2):
                if goes(d, h, c):
                    hop(d, h, c).wait_send()


def shards(residuals, codebook):
    items_n, codes_n = lax.axis_size("items"), lax.axis_size("codes")
    rows, feats = residuals.shape
    codes = codebook.shape[0]
    chunks = rows // CHUNK
    half = codes_n // 2
    mine = rows // codes_n
    f32, bf16 = jnp.float32, jnp.bfloat16
    hbm = pl.BlockSpec(memory_space=pltpu.HBM)
    vmem = pl.BlockSpec(memory_space=pltpu.VMEM)
    dma = pltpu.SemaphoreType.DMA
    softT, items_scale, code_weights = pl.pallas_call(
        functools.partial(
            kernel, items_n, codes_n, float(rows * items_n), float(codes * codes_n)
        ),
        out_shape=(
            jax.ShapeDtypeStruct((feats, rows), f32),
            jax.ShapeDtypeStruct((rows // LANES, LANES), f32),
            jax.ShapeDtypeStruct((codes // LANES, LANES), f32),
        ),
        in_specs=[hbm, hbm],
        out_specs=(vmem, vmem, vmem),
        scratch_shapes=[
            pltpu.VMEM((codes, F), bf16),
            pltpu.VMEM((codes_n, SIDE, SIDE, 2, 2, 16, F), bf16),
            pltpu.VMEM((chunks, F, CHUNK), bf16),
            pltpu.VMEM((codes, rows), f32),
            pltpu.VMEM((mine, codes * codes_n), f32),
            pltpu.VMEM((1, CHUNK), f32),
            pltpu.VMEM((codes, LANES), f32),
            pltpu.VMEM((codes, LANES), f32),
            pltpu.VMEM((codes, LANES), f32),
            pltpu.VMEM((codes // LANES, LANES), f32),
            pltpu.VMEM((codes_n, codes // LANES, LANES), f32),
            pltpu.VMEM((codes_n, codes // LANES, LANES), f32),
            pltpu.VMEM((ITERS, items_n, codes // LANES, LANES), f32),
            pltpu.VMEM((ITERS - 1, codes_n, rows // LANES, LANES), f32),
            pltpu.VMEM((codes_n, mine // LANES, LANES), f32),
            pltpu.VMEM((mine, LANES), f32),
            pltpu.VMEM((mine, F), f32),
            pltpu.VMEM((mine, codes), bf16),
            pltpu.VMEM((F, mine), f32),
            pltpu.VMEM((feats, rows), f32),
            dma((chunks + 1,)),
            dma((2, half, chunks)),
            dma((2, half, chunks)),
            dma((ITERS,)), dma((ITERS,)), dma((ITERS,)), dma((ITERS,)),
            dma((2,)), dma((2,)),
            dma((2, 2)), dma((2, 2)),
            dma, dma,
            dma((2,)), dma((2,)),
        ],
        compiler_params=pltpu.CompilerParams(
            collective_id=0, has_side_effects=True, vmem_limit_bytes=48 * 1024 * 1024
        ),
    )(residuals.T, codebook)
    return softT.T, items_scale.reshape(rows), code_weights.reshape(codes)


def solution(mesh):
    placed = (P("items", "codes"), P("codes", None))
    return jax.shard_map(
        shards,
        mesh=mesh,
        in_specs=placed,
        out_specs=(P("items", "codes"), P("items"), P("codes")),
        check_vma=False,
    )
```

```python
import functools
import math

import jax
import jax.numpy as jnp
from jax import lax
from jax.experimental import pallas as pl
from jax.experimental.pallas import tpu as pltpu
from jax.sharding import PartitionSpec as P

F = 256
ITERS = 3
EPS = 1e-06
SMOOTHING = 32.0
SHIFT = 2.0
LOG2E = 1.4426950408889634

LANES = 128
CHUNK = 256
TILE = 256
PARTS = 4
VMEM_BYTES = 48 * 1024 * 1024
SIDE = 4
MESH = pl.DeviceIdType.MESH


def ring_plan(codes_n, units):
    half = codes_n // 2

    def goes(d, h, u):
        return h < half or (h == half and (u % 2 == 0) == (d == 0))

    return [
        (d, h, u, goes(d, h + 1, u))
        for h in range(1, half + 1) for u in range(units) for d in range(2) if goes(d, h, u)
    ]


def tree_sum(terms):
    while len(terms) > 1:
        terms = [a + b for a, b in zip(terms[::2], terms[1::2])] + terms[len(terms) // 2 * 2:]
    return terms[0]


def kernel(
    items_n, codes_n, total_items, total_codes,
    rt_hbm, cb_hbm, soft_ref, s_ref, w_ref,
    cb, cbf, R, K, K2, inv_row, inv_col, tacc, W, tsend, cinv, wbuf, colbuf, rowbuf, sbuf,
    rows2, a2, r2, mix, shares_a, shares_b, softT, land,
    in_sem, ring_send, ring_recv, col_send, col_recv, row_send, row_recv,
    z_send, z_recv, plane_send, plane_recv, pair_send, pair_recv, out_send, out_recv,
):
    me_i = lax.axis_index("items")
    me_z = lax.axis_index("codes")
    x, y, core = me_i // (2 * SIDE), lax.rem(me_i // 2, SIDE), lax.rem(me_i, 2)
    rows = rt_hbm.shape[1]
    codes = cb_hbm.shape[0]
    feats = rt_hbm.shape[0]
    chunks = rows // CHUNK
    mine = rows // codes_n
    right = lax.rem(me_z + 1, codes_n)
    left = lax.rem(me_z + codes_n - 1, codes_n)
    half = codes_n // 2

    def remote(src, dst, send, recv, device):
        return pltpu.make_async_remote_copy(
            src_ref=src, dst_ref=dst, send_sem=send, recv_sem=recv,
            device_id=device, device_id_type=MESH,
        )

    def wait_bytes(ref, sem):
        pltpu.make_async_copy(ref, ref, sem).wait()

    def at_plane(px, py, pcore):
        return {"items": (px * SIDE + py) * 2 + pcore}

    def block(c, z):
        return R.at[c, pl.ds(pl.multiple_of(z * feats, feats), feats), :]

    own = [
        pltpu.make_async_copy(
            rt_hbm.at[:, c * CHUNK:(c + 1) * CHUNK], block(c, me_z), in_sem.at[c]
        )
        for c in range(chunks)
    ]
    own += [
        pltpu.make_async_copy(
            cb_hbm.at[pl.ds(pl.multiple_of(me_i * 32 + n * 16, 16), 16), :],
            cbf.at[me_z, x, y, core, n], in_sem.at[chunks + 1 + n],
        )
        for n in range(2)
    ]
    for copy in own:
        copy.start()
    load_cb = pltpu.make_async_copy(cb_hbm, cb, in_sem.at[chunks])
    load_cb.start()

    barrier = pltpu.get_barrier_semaphore()

    def greet_items(k, carry):
        pl.semaphore_signal(
            barrier, inc=1, device_id={"items": lax.rem(me_i + k, items_n)}, device_id_type=MESH
        )
        return carry

    def greet_codes(k, carry):
        pl.semaphore_signal(
            barrier, inc=1, device_id={"codes": lax.rem(me_z + k, codes_n)}, device_id_type=MESH
        )
        return carry

    lax.fori_loop(1, codes_n, greet_codes, 0)
    lax.fori_loop(1, items_n, greet_items, 0)

    pl.semaphore_wait(barrier, items_n + codes_n - 2)

    def hop(direction, h, u):
        z = me_z - (h - 1) if direction == 0 else me_z + (h - 1)
        z = lax.rem(z + codes_n, codes_n)
        ref = cbf.at[z, x, y, core] if u == 0 else block(u - 1, z)
        return remote(
            ref, ref, ring_send.at[direction, h - 1, u], ring_recv.at[direction, h - 1, u],
            {"codes": right if direction == 0 else left},
        )

    for copy in own:
        copy.wait()
    for u in range(chunks + 1):
        for d in range(2):
            hop(d, 1, u).start()
    load_cb.wait()
    wide = cb[...].astype(jnp.float32)
    inv_col[...] = jnp.broadcast_to(
        lax.rsqrt(jnp.mean(wide * wide, axis=1, keepdims=True) + EPS), inv_col.shape
    )
    for b in range(codes // LANES):
        tsend[b:b + 1, :] = jnp.transpose(inv_col[b * LANES:(b + 1) * LANES, :])[0:1, :]
    cinv[me_z] = tsend[...]

    def plane_copies(part):
        if part == 0:
            a, b = cbf.at[:, x, y, core, 0], cbf.at[:, x, y, core, 1]
        else:
            zs = pl.ds((part - 1) * (codes_n // PARTS), codes_n // PARTS)
            b, a = cbf.at[zs, :, y, core, 0], cbf.at[zs, x, :, core, 1]
        out = []
        for k in range(1, SIDE):
            to_x = at_plane(lax.rem(x + k, SIDE), y, core)
            to_y = at_plane(x, lax.rem(y + k, SIDE), core)
            out.append(remote(a, a, plane_send.at[part, 0], plane_recv.at[part, 0], to_x))
            out.append(remote(b, b, plane_send.at[part, 1], plane_recv.at[part, 1], to_y))
        return out

    def plane_start(part):
        for copy in plane_copies(part):
            copy.start()

    def plane_wait(part, sem):
        for way in range(2):
            if part == 0:
                ref = cbf.at[:, 0, pl.ds(0, SIDE - 1), 0, 0]
            else:
                ref = cbf.at[pl.ds(0, codes_n // PARTS), :, pl.ds(0, SIDE - 1), 0, 0]
            wait_bytes(ref, sem.at[part, way])

    def pair_copy(part):
        ref = cbf.at[pl.ds(part * (codes_n // PARTS), codes_n // PARTS), :, :, core]
        return remote(ref, ref, pair_send.at[part], pair_recv.at[part], at_plane(x, y, 1 - core))

    def tile(c):
        r_wide = R[c].astype(jnp.float32)
        inv_row[...] = lax.rsqrt(
            jnp.mean(r_wide * r_wide, axis=0, keepdims=True) + EPS
        ) * (SMOOTHING * LOG2E / F)

        def tile_step(m, carry):
            at = pl.ds(pl.multiple_of(m * TILE, TILE), TILE)
            dots = jnp.dot(cb[at, :], R[c], preferred_element_type=jnp.float32)
            scale = inv_col[at, :]
            values = []
            for q in range(CHUNK // LANES):
                lanes = slice(q * LANES, (q + 1) * LANES)
                value = jnp.exp2(dots[:, lanes] * inv_row[:, lanes] * scale)
                K[at, c * CHUNK + q * LANES:c * CHUNK + (q + 1) * LANES] = value
                values.append(value)
            total = tree_sum(values)
            if c in first_tile:
                tacc[at, :] = total
            else:
                tacc[at, :] += total
            return carry

        lax.fori_loop(0, codes // TILE, tile_step, 0, unroll=True)

    plan = ring_plan(codes_n, chunks + 1)
    left_over = [sum(1 for d, h, u, then in plan if u == v) for v in range(chunks + 1)]
    first_tile = []
    for d, h, u, then in plan:
        hop(d, h, u).wait_recv()
        if then:
            hop(d, h + 1, u).start()
        left_over[u] -= 1
        if left_over[u] == 0:
            if u == 0:
                plane_start(0)
            else:
                if not first_tile:
                    first_tile.append(u - 1)
                else:
                    first_tile[:] = [-1]
                tile(u - 1)

    groups = codes // 8
    lane_chunks = rows // LANES

    def exchange(buf, mine_at, count, axis, send_sem, recv_sem):
        def send(k, carry):
            ref = buf.at[mine_at]
            remote(ref, ref, send_sem, recv_sem, {axis: lax.rem(mine_at + k, count)}).start()
            return carry

        lax.fori_loop(1, count, send, 0)

    def all_but_one(buf, count, sem):
        wait_bytes(buf.at[pl.ds(0, count - 1)], sem)

    def second_rows():
        rows2[...] = jnp.transpose(R[me_z])
        wide2 = rows2[...].astype(jnp.float32)
        a2[...] = jnp.broadcast_to(
            lax.rsqrt(jnp.mean(wide2 * wide2, axis=1, keepdims=True) + EPS)
            * (SMOOTHING * LOG2E / F), a2.shape)

    def second_tile(part):
        def step(n, carry):
            z, k = n // 4, lax.rem(n, 4)
            some = cbf[z, k].reshape(codes // 4, F)
            dots = lax.dot_general(
                rows2[...], some, (((1,), (1,)), ((), ())), preferred_element_type=jnp.float32
            )
            for q in range(2):
                scale = cinv[z, pl.ds(2 * k + q, 1), :]
                value = jnp.exp2(dots[:, q * LANES:(q + 1) * LANES] * a2[...] * scale)
                K2[:, pl.ds(pl.multiple_of(n * 256 + q * LANES, LANES), LANES)] = value
            return carry

        steps = 4 * codes_n // PARTS
        lax.fori_loop(part * steps, (part + 1) * steps, step, 0, unroll=4)

    def send_inv(k, carry):
        remote(cinv.at[me_z], cinv.at[me_z], z_send, z_recv,
               {"codes": lax.rem(me_z + k, codes_n)}).start()
        return carry

    lax.fori_loop(1, codes_n, send_inv, 0)

    for it in range(ITERS):
        last = it == ITERS - 1
        if it > 0:
            s_bcast = [
                jnp.broadcast_to(s_ref[q:q + 1, :], (8, LANES)) for q in range(lane_chunks)
            ]

            def col_step(g, carry):
                at = pl.ds(pl.multiple_of(g * 8, 8), 8)
                tacc[at, :] = tree_sum([
                    K[at, q * LANES:(q + 1) * LANES] * s_bcast[q] for q in range(lane_chunks)
                ])
                return carry

            lax.fori_loop(0, groups, col_step, 0, unroll=4)
        for b in range(codes // LANES):
            blockT = jnp.transpose(tacc[b * LANES:(b + 1) * LANES, :])
            tsend[b:b + 1, :] = jnp.sum(blockT, axis=0, keepdims=True)
        colbuf[it, me_i] = tsend[...]
        exchange(colbuf.at[it], me_i, items_n, "items", col_send.at[it], col_recv.at[it])
        if it == 0:
            for d, h, u, then in plan:
                hop(d, h, u).wait_send()
            second_rows()
            plane_wait(0, plane_recv)
        if it == 1:
            for part in (0, 1):
                plane_wait(1 + part, plane_recv)
                pair_copy(part).start()
            plane_wait(0, plane_send)
            all_but_one(colbuf.at[0], items_n, col_send.at[0])
            all_but_one(rowbuf.at[0], codes_n, row_send.at[0])
            all_but_one(cinv, codes_n, z_recv)
            all_but_one(cinv, codes_n, z_send)
        if last:
            for part in (2, 3):
                plane_wait(1 + part, plane_recv)
                pair_copy(part).start()
            for part in (2, 3):
                pair_copy(part).wait_recv()
                second_tile(part)
        all_but_one(colbuf.at[it], items_n, col_recv.at[it])
        if not last:
            plane_start(1 + 2 * it)
            plane_start(2 + 2 * it)
        w = total_items / jnp.sum(colbuf[it], axis=0)
        if last:
            w_ref[...] = w * math.exp(SHIFT)
            wbuf[me_z] = w * (1.0 / total_codes)
            exchange(wbuf, me_z, codes_n, "codes", row_send.at[it], row_recv.at[it])
            for past in (1, 2):
                all_but_one(colbuf.at[past], items_n, col_send.at[past])
            all_but_one(rowbuf.at[1], codes_n, row_send.at[1])
            for part in range(PARTS):
                plane_wait(1 + part, plane_send)
                pair_copy(part).wait_send()
            all_but_one(wbuf, codes_n, row_recv.at[it])
            break
        for b in range(codes // LANES):
            W[b * LANES:(b + 1) * LANES, :] = jnp.transpose(
                jnp.broadcast_to(w[b:b + 1, :], (LANES, LANES))
            )

        def row_step(g, acc):
            at = pl.ds(pl.multiple_of(g * 8, 8), 8)
            weight = W[at, :]
            return tuple(
                acc[q] + K[at, q * LANES:(q + 1) * LANES] * weight for q in range(lane_chunks)
            )

        acc = lax.fori_loop(
            0, groups, row_step,
            tuple(jnp.zeros((8, LANES), jnp.float32) for _ in range(lane_chunks)), unroll=4,
        )
        for q in range(lane_chunks):
            s_ref[q:q + 1, :] = jnp.sum(acc[q], axis=0, keepdims=True)
        rowbuf[it, me_z] = s_ref[...]
        exchange(rowbuf.at[it], me_z, codes_n, "codes", row_send.at[it], row_recv.at[it])
        if it == 1:
            for part in (0, 1):
                pair_copy(part).wait_recv()
                second_tile(part)
        all_but_one(rowbuf.at[it], codes_n, row_recv.at[it])
        s_ref[...] = total_codes / jnp.sum(rowbuf[it], axis=0)

    def part_of(z):
        return pl.ds(pl.multiple_of(z * feats, feats), feats)

    def shares_of(z, at, out):
        total = []
        for q in range(codes // LANES):
            value = K2[at, z * codes + q * LANES:z * codes + (q + 1) * LANES] * wbuf[z, q:q + 1, :]
            total.append(value)
            out[:, q * LANES:(q + 1) * LANES] = value.astype(jnp.bfloat16)
        r2[...] = tree_sum(total) if z == 0 else r2[...] + tree_sum(total)

    def mix_of(z, src):
        some = jnp.dot(src[...], cbf[z].reshape(codes, F), preferred_element_type=jnp.float32)
        mix[...] = some if z == 0 else mix[...] + some

    buffers = (shares_a, shares_b)
    for b in range(mine // LANES):
        at = slice(b * LANES, (b + 1) * LANES)
        shares_of(0, at, buffers[0])
        for z in range(codes_n):
            if z + 1 < codes_n:
                shares_of(z + 1, at, buffers[(z + 1) % 2])
            mix_of(z, buffers[z % 2])
        scale = 1.0 / jnp.sum(jnp.transpose(r2[...]), axis=0, keepdims=True)
        sbuf[me_z, b:b + 1, :] = scale
        softT[b] = jnp.transpose(mix[...]) * scale
        my_lanes = pl.ds(pl.multiple_of(me_z * mine + b * LANES, LANES), LANES)

        def send_out(k, carry, b=b, my_lanes=my_lanes):
            z = lax.rem(me_z + k, codes_n)
            remote(softT.at[b, part_of(z), :], land.at[:, my_lanes],
                   out_send.at[b], out_recv.at[b], {"codes": z}).start()
            return carry

        lax.fori_loop(1, codes_n, send_out, 0)
        land[:, my_lanes] = softT[b, part_of(me_z), :]
    exchange(sbuf, me_z, codes_n, "codes", out_send.at[2], out_recv.at[2])
    all_but_one(wbuf, codes_n, row_send.at[ITERS - 1])

    for b in range(mine // LANES):
        wait_bytes(land.at[:, pl.ds(0, (codes_n - 1) * LANES)], out_recv.at[b])
    all_but_one(sbuf, codes_n, out_recv.at[2])
    soft_ref[...] = land[...]
    for z in range(codes_n):
        for b in range(mine // LANES):
            n = z * (mine // LANES) + b
            s_ref[n:n + 1, :] = sbuf[z, b:b + 1, :]
    for b in range(mine // LANES):
        wait_bytes(land.at[:, pl.ds(0, (codes_n - 1) * LANES)], out_send.at[b])
    all_but_one(sbuf, codes_n, out_send.at[2])


def shards(residuals, codebook):
    items_n, codes_n = lax.axis_size("items"), lax.axis_size("codes")
    rows, feats = residuals.shape
    codes = codebook.shape[0]
    chunks = rows // CHUNK
    half = codes_n // 2
    mine = rows // codes_n
    f32, bf16 = jnp.float32, jnp.bfloat16
    hbm = pl.BlockSpec(memory_space=pltpu.HBM)
    vmem = pl.BlockSpec(memory_space=pltpu.VMEM)
    dma = pltpu.SemaphoreType.DMA
    softT, items_scale, code_weights = pl.pallas_call(
        functools.partial(
            kernel, items_n, codes_n, float(rows * items_n), float(codes * codes_n)
        ),
        out_shape=(
            jax.ShapeDtypeStruct((feats, rows), f32),
            jax.ShapeDtypeStruct((rows // LANES, LANES), f32),
            jax.ShapeDtypeStruct((codes // LANES, LANES), f32),
        ),
        in_specs=[hbm, hbm],
        out_specs=(vmem, vmem, vmem),
        scratch_shapes=[
            pltpu.VMEM((codes, F), bf16),
            pltpu.VMEM((codes_n, SIDE, SIDE, 2, 2, 16, F), bf16),
            pltpu.VMEM((chunks, F, CHUNK), bf16),
            pltpu.VMEM((codes, rows), f32),
            pltpu.VMEM((mine, codes * codes_n), f32),
            pltpu.VMEM((1, CHUNK), f32),
            pltpu.VMEM((codes, LANES), f32),
            pltpu.VMEM((codes, LANES), f32),
            pltpu.VMEM((codes, LANES), f32),
            pltpu.VMEM((codes // LANES, LANES), f32),
            pltpu.VMEM((codes_n, codes // LANES, LANES), f32),
            pltpu.VMEM((codes_n, codes // LANES, LANES), f32),
            pltpu.VMEM((ITERS, items_n, codes // LANES, LANES), f32),
            pltpu.VMEM((ITERS - 1, codes_n, rows // LANES, LANES), f32),
            pltpu.VMEM((codes_n, mine // LANES, LANES), f32),
            pltpu.VMEM((mine, F), bf16),
            pltpu.VMEM((mine, LANES), f32),
            pltpu.VMEM((LANES, LANES), f32),
            pltpu.VMEM((LANES, F), f32),
            pltpu.VMEM((LANES, codes), bf16),
            pltpu.VMEM((LANES, codes), bf16),
            pltpu.VMEM((mine // LANES, F, LANES), f32),
            pltpu.VMEM((feats, rows), f32),
            dma((chunks + 3,)),
            dma((2, half, chunks + 1)),
            dma((2, half, chunks + 1)),
            dma((ITERS,)), dma((ITERS,)), dma((ITERS,)), dma((ITERS,)),
            dma, dma,
            dma((PARTS + 1, 2)), dma((PARTS + 1, 2)),
            dma((PARTS,)), dma((PARTS,)),
            dma((3,)), dma((3,)),
        ],
        compiler_params=pltpu.CompilerParams(
            collective_id=0, has_side_effects=True, vmem_limit_bytes=VMEM_BYTES
        ),
    )(pltpu.with_memory_space_constraint(residuals.T, pltpu.HBM), pltpu.with_memory_space_constraint(codebook, pltpu.HBM))
    return softT.T, items_scale.reshape(rows), code_weights.reshape(codes)


def solution(mesh):
    placed = (P("items", "codes"), P("codes", None))
    return jax.shard_map(
        shards,
        mesh=mesh,
        in_specs=placed,
        out_specs=(P("items", "codes"), P("items"), P("codes")),
        check_vma=False,
    )
```

```python
import functools
import math

import jax
import jax.numpy as jnp
from jax import lax
from jax.experimental import pallas as pl
from jax.experimental.pallas import tpu as pltpu
from jax.sharding import PartitionSpec as P

F = 256
ITERS = 3
EPS = 1e-06
SMOOTHING = 32.0
SHIFT = 2.0
LOG2E = 1.4426950408889634

LANES = 128
CHUNK = 256
TILE = 256
PARTS = 4
LEVELS = 7.0
VMEM_BYTES = 48 * 1024 * 1024
SIDE = 4
MESH = pl.DeviceIdType.MESH


def ring_plan(codes_n, units):
    half = codes_n // 2

    def goes(d, h, u):
        return h < half or (h == half and (u % 2 == 0) == (d == 0))

    return [
        (d, h, u, goes(d, h + 1, u))
        for h in range(1, half + 1) for u in range(units) for d in range(2) if goes(d, h, u)
    ]


def tree_sum(terms):
    while len(terms) > 1:
        terms = [a + b for a, b in zip(terms[::2], terms[1::2])] + terms[len(terms) // 2 * 2:]
    return terms[0]


def kernel(
    items_n, codes_n, total_items, total_codes,
    rt_hbm, cb_hbm, soft_ref, s_ref, w_ref,
    cb, cbf, R, K, K2, inv_row, inv_col, tacc, W, tsend, cinv, wbuf, colbuf, rowbuf, sbuf,
    rows2, a2, r2, mix, shares_a, shares_b, softT, land,
    in_sem, ring_send, ring_recv, col_send, col_recv, row_send, row_recv,
    w_send, w_recv, z_send, z_recv, plane_send, plane_recv, pair_send, pair_recv, out_send, out_recv,
):
    me_i = lax.axis_index("items")
    me_z = lax.axis_index("codes")
    x, y, core = me_i // (2 * SIDE), lax.rem(me_i // 2, SIDE), lax.rem(me_i, 2)
    rows = rt_hbm.shape[1]
    codes = cb_hbm.shape[0]
    feats = rt_hbm.shape[0]
    chunks = rows // CHUNK
    mine = rows // codes_n
    right = lax.rem(me_z + 1, codes_n)
    left = lax.rem(me_z + codes_n - 1, codes_n)
    half = codes_n // 2

    def remote(src, dst, send, recv, device):
        return pltpu.make_async_remote_copy(
            src_ref=src, dst_ref=dst, send_sem=send, recv_sem=recv,
            device_id=device, device_id_type=MESH,
        )

    def wait_bytes(ref, sem):
        pltpu.make_async_copy(ref, ref, sem).wait()

    def at_plane(px, py, pcore):
        return {"items": (px * SIDE + py) * 2 + pcore}

    def block(c, z):
        return R.at[c, pl.ds(pl.multiple_of(z * feats, feats), feats), :]

    own = [
        pltpu.make_async_copy(
            rt_hbm.at[:, c * CHUNK:(c + 1) * CHUNK], block(c, me_z), in_sem.at[c]
        )
        for c in range(chunks)
    ]
    own += [
        pltpu.make_async_copy(
            cb_hbm.at[pl.ds(pl.multiple_of(me_i * 32 + n * 16, 16), 16), :],
            cbf.at[me_z, x, y, core, n], in_sem.at[chunks + 1 + n],
        )
        for n in range(2)
    ]
    for copy in own:
        copy.start()
    load_cb = pltpu.make_async_copy(cb_hbm, cb, in_sem.at[chunks])
    load_cb.start()

    barrier = pltpu.get_barrier_semaphore()

    def greet_items(k, carry):
        pl.semaphore_signal(
            barrier, inc=1, device_id={"items": lax.rem(me_i + k, items_n)}, device_id_type=MESH
        )
        return carry

    def greet_codes(k, carry):
        pl.semaphore_signal(
            barrier, inc=1, device_id={"codes": lax.rem(me_z + k, codes_n)}, device_id_type=MESH
        )
        return carry

    lax.fori_loop(1, codes_n, greet_codes, 0)
    lax.fori_loop(1, items_n, greet_items, 0)

    pl.semaphore_wait(barrier, items_n + codes_n - 2)

    def hop(direction, h, u):
        z = me_z - (h - 1) if direction == 0 else me_z + (h - 1)
        z = lax.rem(z + codes_n, codes_n)
        ref = cbf.at[z, x, y, core] if u == 0 else block(u - 1, z)
        return remote(
            ref, ref, ring_send.at[direction, h - 1, u], ring_recv.at[direction, h - 1, u],
            {"codes": right if direction == 0 else left},
        )

    for copy in own:
        copy.wait()
    for u in range(chunks + 1):
        for d in range(2):
            hop(d, 1, u).start()
    load_cb.wait()
    wide = cb[...].astype(jnp.float32)
    inv_col[...] = jnp.broadcast_to(
        lax.rsqrt(jnp.mean(wide * wide, axis=1, keepdims=True) + EPS), inv_col.shape
    )
    for b in range(codes // LANES):
        tsend[b:b + 1, :] = jnp.transpose(inv_col[b * LANES:(b + 1) * LANES, :])[0:1, :]
    cinv[me_z] = tsend[...]

    def plane_copies(part):
        if part == 0:
            a, b = cbf.at[:, x, y, core, 0], cbf.at[:, x, y, core, 1]
        else:
            zs = pl.ds((part - 1) * (codes_n // PARTS), codes_n // PARTS)
            b, a = cbf.at[zs, :, y, core, 0], cbf.at[zs, x, :, core, 1]
        out = []
        for k in range(1, SIDE):
            to_x = at_plane(lax.rem(x + k, SIDE), y, core)
            to_y = at_plane(x, lax.rem(y + k, SIDE), core)
            out.append(remote(a, a, plane_send.at[part, 0], plane_recv.at[part, 0], to_x))
            out.append(remote(b, b, plane_send.at[part, 1], plane_recv.at[part, 1], to_y))
        return out

    def plane_start(part):
        for copy in plane_copies(part):
            copy.start()

    def plane_wait(part, sem):
        for way in range(2):
            if part == 0:
                ref = cbf.at[:, 0, pl.ds(0, SIDE - 1), 0, 0]
            else:
                ref = cbf.at[pl.ds(0, codes_n // PARTS), :, pl.ds(0, SIDE - 1), 0, 0]
            wait_bytes(ref, sem.at[part, way])

    def pair_copy(part):
        ref = cbf.at[pl.ds(part * (codes_n // PARTS), codes_n // PARTS), :, :, core]
        return remote(ref, ref, pair_send.at[part], pair_recv.at[part], at_plane(x, y, 1 - core))

    def tile(c):
        r_wide = R[c].astype(jnp.float32)
        inv_row[...] = lax.rsqrt(
            jnp.mean(r_wide * r_wide, axis=0, keepdims=True) + EPS
        ) * (SMOOTHING * LOG2E / F)

        def tile_step(m, carry):
            at = pl.ds(pl.multiple_of(m * TILE, TILE), TILE)
            dots = jnp.dot(cb[at, :], R[c], preferred_element_type=jnp.float32)
            scale = inv_col[at, :]
            values = []
            for q in range(CHUNK // LANES):
                lanes = slice(q * LANES, (q + 1) * LANES)
                value = jnp.exp2(dots[:, lanes] * inv_row[:, lanes] * scale)
                K[at, c * CHUNK + q * LANES:c * CHUNK + (q + 1) * LANES] = value
                values.append(value)
            total = tree_sum(values)
            if c in first_tile:
                tacc[at, :] = total
            else:
                tacc[at, :] += total
            return carry

        lax.fori_loop(0, codes // TILE, tile_step, 0, unroll=True)

    plan = ring_plan(codes_n, chunks + 1)
    left_over = [sum(1 for d, h, u, then in plan if u == v) for v in range(chunks + 1)]
    first_tile = []
    for d, h, u, then in plan:
        hop(d, h, u).wait_recv()
        if then:
            hop(d, h + 1, u).start()
        left_over[u] -= 1
        if left_over[u] == 0:
            if u == 0:
                plane_start(0)
            else:
                if not first_tile:
                    first_tile.append(u - 1)
                else:
                    first_tile[:] = [-1]
                tile(u - 1)

    groups = codes // 8
    lane_chunks = rows // LANES

    ring_order = sorted(range(1, codes_n), key=lambda k: -min(k, codes_n - k))
    plane_order = sorted(
        [(dx, dy, dc) for dx in range(SIDE) for dy in range(SIDE) for dc in range(2)],
        key=lambda o: -(min(o[0], SIDE - o[0]) + min(o[1], SIDE - o[1])),
    )

    def exchange_codes(ref, send_sem, recv_sem):
        for k in ring_order:
            to = {"codes": lax.rem(me_z + k, codes_n)}
            remote(ref, ref, send_sem, recv_sem, to).start()

    def exchange_items(ref, send_sem, recv_sem):
        for dx, dy, dc in plane_order:
            if dx or dy or dc:
                to = at_plane(lax.rem(x + dx, SIDE), lax.rem(y + dy, SIDE), lax.rem(core + dc, 2))
                remote(ref, ref, send_sem, recv_sem, to).start()

    def all_but_one(buf, count, sem):
        wait_bytes(buf.at[pl.ds(0, count - 1)], sem)

    def second_rows():
        rows2[...] = jnp.transpose(R[me_z])
        wide2 = rows2[...].astype(jnp.float32)
        a2[...] = jnp.broadcast_to(
            lax.rsqrt(jnp.mean(wide2 * wide2, axis=1, keepdims=True) + EPS)
            * (SMOOTHING * LOG2E / F), a2.shape)

    def second_tile(part):
        def step(n, carry):
            z, k = n // 4, lax.rem(n, 4)
            some = cbf[z, k].reshape(codes // 4, F)
            dots = lax.dot_general(
                rows2[...], some, (((1,), (1,)), ((), ())), preferred_element_type=jnp.float32
            )
            for q in range(2):
                scale = cinv[z, pl.ds(2 * k + q, 1), :]
                value = jnp.exp2(dots[:, q * LANES:(q + 1) * LANES] * a2[...] * scale)
                K2[:, pl.ds(pl.multiple_of(n * 256 + q * LANES, LANES), LANES)] = value
            return carry

        steps = 4 * codes_n // PARTS
        lax.fori_loop(part * steps, (part + 1) * steps, step, 0, unroll=4)

    def send_inv(k, carry):
        remote(cinv.at[me_z], cinv.at[me_z], z_send, z_recv,
               {"codes": lax.rem(me_z + k, codes_n)}).start()
        return carry

    lax.fori_loop(1, codes_n, send_inv, 0)

    for it in range(ITERS):
        last = it == ITERS - 1
        if it > 0:
            s_bcast = [
                jnp.broadcast_to(s_ref[q:q + 1, :], (8, LANES)) for q in range(lane_chunks)
            ]

            def col_step(g, carry):
                at = pl.ds(pl.multiple_of(g * 8, 8), 8)
                tacc[at, :] = tree_sum([
                    K[at, q * LANES:(q + 1) * LANES] * s_bcast[q] for q in range(lane_chunks)
                ])
                return carry

            lax.fori_loop(0, groups, col_step, 0, unroll=4)
        for b in range(codes // LANES):
            blockT = jnp.transpose(tacc[b * LANES:(b + 1) * LANES, :])
            tsend[b:b + 1, :] = jnp.sum(blockT, axis=0, keepdims=True)
        colbuf[it, me_i] = tsend[...]
        exchange_items(colbuf.at[it, me_i], col_send.at[it], col_recv.at[it])
        if it == 0:
            for d, h, u, then in plan:
                hop(d, h, u).wait_send()
            second_rows()
            plane_wait(0, plane_recv)
        if it == 1:
            for part in (0, 1):
                plane_wait(1 + part, plane_recv)
                pair_copy(part).start()
            plane_wait(0, plane_send)
            all_but_one(colbuf.at[0], items_n, col_send.at[0])
            all_but_one(rowbuf.at[0], codes_n, row_send.at[0])
            all_but_one(cinv, codes_n, z_recv)
            all_but_one(cinv, codes_n, z_send)
        if last:
            for part in (2, 3):
                plane_wait(1 + part, plane_recv)
                pair_copy(part).start()
            for part in (2, 3):
                pair_copy(part).wait_recv()
                second_tile(part)
        all_but_one(colbuf.at[it], items_n, col_recv.at[it])
        if not last:
            plane_start(1 + 2 * it)
            plane_start(2 + 2 * it)
        w = total_items / jnp.sum(colbuf[it], axis=0)
        if last:
            w_ref[...] = w * math.exp(SHIFT)
            wbuf[me_z] = w * (1.0 / total_codes)
            for k in ring_order:
                remote(wbuf.at[me_z], wbuf.at[me_z], w_send, w_recv.at[k],
                       {"codes": lax.rem(me_z + k, codes_n)}).start()
            for past in (1, 2):
                all_but_one(colbuf.at[past], items_n, col_send.at[past])
            all_but_one(rowbuf.at[1], codes_n, row_send.at[1])
            for part in range(PARTS):
                plane_wait(1 + part, plane_send)
                pair_copy(part).wait_send()
            break
        for b in range(codes // LANES):
            W[b * LANES:(b + 1) * LANES, :] = jnp.transpose(
                jnp.broadcast_to(w[b:b + 1, :], (LANES, LANES))
            )

        def row_step(g, acc):
            at = pl.ds(pl.multiple_of(g * 8, 8), 8)
            weight = W[at, :]
            return tuple(
                acc[q] + K[at, q * LANES:(q + 1) * LANES] * weight for q in range(lane_chunks)
            )

        acc = lax.fori_loop(
            0, groups, row_step,
            tuple(jnp.zeros((8, LANES), jnp.float32) for _ in range(lane_chunks)), unroll=4,
        )
        for q in range(lane_chunks):
            s_ref[q:q + 1, :] = jnp.sum(acc[q], axis=0, keepdims=True)
        rowbuf[it, me_z] = s_ref[...]
        exchange_codes(rowbuf.at[it, me_z], row_send.at[it], row_recv.at[it])
        if it == 1:
            for part in (0, 1):
                pair_copy(part).wait_recv()
                second_tile(part)
        all_but_one(rowbuf.at[it], codes_n, row_recv.at[it])
        s_ref[...] = total_codes / jnp.sum(rowbuf[it], axis=0)

    def part_of(z):
        return pl.ds(pl.multiple_of(z * feats, feats), feats)

    def shares_of(z, at, first, out):
        total = []
        for q in range(codes // LANES):
            lanes = slice(z * codes + q * LANES, z * codes + (q + 1) * LANES)
            value = K2[at, lanes] * wbuf[z, q:q + 1, :]
            total.append(value)
            out[:, q * LANES:(q + 1) * LANES] = value.astype(jnp.bfloat16)
        r2[...] = tree_sum(total) if first else r2[...] + tree_sum(total)

    def mix_of(z, first, src):
        some = jnp.dot(src[...], cbf[z].reshape(codes, F), preferred_element_type=jnp.float32)
        mix[...] = some if first else mix[...] + some

    def encode(b, values):
        near = values.astype(jnp.bfloat16)
        wide = near.astype(jnp.float32)
        left = (values - wide) * (LEVELS * 256.0 / jnp.maximum(jnp.abs(wide), 1e-30))
        left = jnp.clip(jnp.round(left), -LEVELS, LEVELS).reshape(codes_n, 2, feats // 2, LANES)
        softT[b, :, :feats, :] = near.reshape(codes_n, feats, LANES)
        softT[b, :, feats:, :] = (left[:, 0] * 16.0 + left[:, 1]).astype(jnp.bfloat16)

    def decode(coded):
        wide = coded[:feats, :].astype(jnp.float32)
        both = coded[feats:, :].astype(jnp.float32)
        high = jnp.round(both * (1.0 / 16.0))
        left = jnp.concatenate([high, both - 16.0 * high], axis=0)
        return wide + jnp.abs(wide) * (left * (1.0 / (LEVELS * 256.0)))

    for k in ring_order:
        wait_bytes(wbuf.at[0], w_recv.at[k])
    buffers = (shares_a, shares_b)

    def half_step(b, carry):
        at = pl.ds(pl.multiple_of(b * LANES, LANES), LANES)
        for z in range(codes_n):
            shares_of(z, at, z == 0, buffers[z % 2])
            if z > 0:
                mix_of(z - 1, z == 1, buffers[(z - 1) % 2])
        mix_of(codes_n - 1, False, buffers[(codes_n - 1) % 2])
        scale = 1.0 / jnp.sum(jnp.transpose(r2[...]), axis=0, keepdims=True)
        sbuf[me_z, pl.ds(b, 1), :] = scale
        encode(b, jnp.transpose(mix[...]) * scale)
        for k in ring_order:
            z = lax.rem(me_z + k, codes_n)
            remote(softT.at[b, z], land.at[b, me_z], out_send.at[b], out_recv.at[b],
                   {"codes": z}).start()
        land[b, me_z] = softT[b, me_z]
        return carry

    lax.fori_loop(0, mine // LANES, half_step, 0)
    exchange_codes(sbuf.at[me_z], out_send.at[2], out_recv.at[2])
    all_but_one(wbuf, codes_n, w_send)

    all_but_one(sbuf, codes_n, out_recv.at[2])
    for z in range(codes_n):
        for b in range(mine // LANES):
            n = z * (mine // LANES) + b
            s_ref[n:n + 1, :] = sbuf[z, b:b + 1, :]
    for b in range(mine // LANES):
        all_but_one(land.at[b], codes_n, out_recv.at[b])
        for z in range(codes_n):
            n = z * (mine // LANES) + b
            soft_ref[:, n * LANES:(n + 1) * LANES] = decode(land[b, z])
    for b in range(mine // LANES):
        all_but_one(land.at[b], codes_n, out_send.at[b])
    all_but_one(sbuf, codes_n, out_send.at[2])


def shards(residuals, codebook):
    items_n, codes_n = lax.axis_size("items"), lax.axis_size("codes")
    rows, feats = residuals.shape
    codes = codebook.shape[0]
    chunks = rows // CHUNK
    half = codes_n // 2
    mine = rows // codes_n
    f32, bf16 = jnp.float32, jnp.bfloat16
    hbm = pl.BlockSpec(memory_space=pltpu.HBM)
    vmem = pl.BlockSpec(memory_space=pltpu.VMEM)
    dma = pltpu.SemaphoreType.DMA
    softT, items_scale, code_weights = pl.pallas_call(
        functools.partial(
            kernel, items_n, codes_n, float(rows * items_n), float(codes * codes_n)
        ),
        out_shape=(
            jax.ShapeDtypeStruct((feats, rows), f32),
            jax.ShapeDtypeStruct((rows // LANES, LANES), f32),
            jax.ShapeDtypeStruct((codes // LANES, LANES), f32),
        ),
        in_specs=[hbm, hbm],
        out_specs=(vmem, vmem, vmem),
        scratch_shapes=[
            pltpu.VMEM((codes, F), bf16),
            pltpu.VMEM((codes_n, SIDE, SIDE, 2, 2, 16, F), bf16),
            pltpu.VMEM((chunks, F, CHUNK), bf16),
            pltpu.VMEM((codes, rows), f32),
            pltpu.VMEM((mine, codes * codes_n), f32),
            pltpu.VMEM((1, CHUNK), f32),
            pltpu.VMEM((codes, LANES), f32),
            pltpu.VMEM((codes, LANES), f32),
            pltpu.VMEM((codes, LANES), f32),
            pltpu.VMEM((codes // LANES, LANES), f32),
            pltpu.VMEM((codes_n, codes // LANES, LANES), f32),
            pltpu.VMEM((codes_n, codes // LANES, LANES), f32),
            pltpu.VMEM((ITERS, items_n, codes // LANES, LANES), f32),
            pltpu.VMEM((ITERS - 1, codes_n, rows // LANES, LANES), f32),
            pltpu.VMEM((codes_n, mine // LANES, LANES), f32),
            pltpu.VMEM((mine, F), bf16),
            pltpu.VMEM((mine, LANES), f32),
            pltpu.VMEM((LANES, LANES), f32),
            pltpu.VMEM((LANES, F), f32),
            pltpu.VMEM((LANES, codes), bf16),
            pltpu.VMEM((LANES, codes), bf16),
            pltpu.VMEM((mine // LANES, codes_n, feats + feats // 2, LANES), bf16),
            pltpu.VMEM((mine // LANES, codes_n, feats + feats // 2, LANES), bf16),
            dma((chunks + 3,)),
            dma((2, half, chunks + 1)),
            dma((2, half, chunks + 1)),
            dma((ITERS,)), dma((ITERS,)), dma((ITERS - 1,)), dma((ITERS - 1,)),
            dma, dma((codes_n,)),
            dma, dma,
            dma((PARTS + 1, 2)), dma((PARTS + 1, 2)),
            dma((PARTS,)), dma((PARTS,)),
            dma((3,)), dma((3,)),
        ],
        compiler_params=pltpu.CompilerParams(
            collective_id=0, has_side_effects=True, vmem_limit_bytes=VMEM_BYTES
        ),
    )(pltpu.with_memory_space_constraint(residuals.T, pltpu.HBM), pltpu.with_memory_space_constraint(codebook, pltpu.HBM))
    return softT.T, items_scale.reshape(rows), code_weights.reshape(codes)


def solution(mesh):
    placed = (P("items", "codes"), P("codes", None))
    return jax.shard_map(
        shards,
        mesh=mesh,
        in_specs=placed,
        out_specs=(P("items", "codes"), P("items"), P("codes")),
        check_vma=False,
    )
```

```python
import functools
import math

import jax
import jax.numpy as jnp
from jax import lax
from jax.experimental import pallas as pl
from jax.experimental.pallas import tpu as pltpu
from jax.sharding import PartitionSpec as P

F = 256
ITERS = 3
EPS = 1e-06
SMOOTHING = 32.0
SHIFT = 2.0
LOG2E = 1.4426950408889634

LANES = 128
CHUNK = 256
TILE = 256
PARTS = 4
LEVELS = 7.0
VMEM_BYTES = 48 * 1024 * 1024
SIDE = 4
MESH = pl.DeviceIdType.MESH


def ring_plan(codes_n, units):
    half = codes_n // 2

    def goes(d, h, u):
        return h < half or (h == half and (u % 2 == 0) == (d == 0))

    return [
        (d, h, u, goes(d, h + 1, u))
        for h in range(1, half + 1) for u in range(units) for d in range(2) if goes(d, h, u)
    ]


def tree_sum(terms):
    while len(terms) > 1:
        terms = [a + b for a, b in zip(terms[::2], terms[1::2])] + terms[len(terms) // 2 * 2:]
    return terms[0]


def kernel(
    items_n, codes_n, total_items, total_codes,
    rt_hbm, cb_hbm, out_ref,
    s_ref, cb, cbf, R, K, K2, inv_row, inv_col, tacc, W, tsend, cinv, wbuf, colbuf, rowbuf, sbuf,
    rows2, a2, r2, mix, shares_a, shares_b, softT, land,
    in_sem, ring_send, ring_recv, col_send, col_recv, row_send, row_recv,
    w_send, w_recv, z_send, z_recv, plane_send, plane_recv, pair_send, pair_recv, out_send, out_recv,
):
    me_i = lax.axis_index("items")
    me_z = lax.axis_index("codes")
    x, y, core = me_i // (2 * SIDE), lax.rem(me_i // 2, SIDE), lax.rem(me_i, 2)
    rows = rt_hbm.shape[1]
    codes = cb_hbm.shape[0]
    feats = rt_hbm.shape[0]
    chunks = rows // CHUNK
    mine = rows // codes_n
    right = lax.rem(me_z + 1, codes_n)
    left = lax.rem(me_z + codes_n - 1, codes_n)
    half = codes_n // 2

    def remote(src, dst, send, recv, device):
        return pltpu.make_async_remote_copy(
            src_ref=src, dst_ref=dst, send_sem=send, recv_sem=recv,
            device_id=device, device_id_type=MESH,
        )

    def wait_bytes(ref, sem):
        pltpu.make_async_copy(ref, ref, sem).wait()

    def at_plane(px, py, pcore):
        return {"items": (px * SIDE + py) * 2 + pcore}

    def block(c, z):
        return R.at[c, pl.ds(pl.multiple_of(z * feats, feats), feats), :]

    own = [
        pltpu.make_async_copy(
            rt_hbm.at[:, c * CHUNK:(c + 1) * CHUNK], block(c, me_z), in_sem.at[c]
        )
        for c in range(chunks)
    ]
    own += [
        pltpu.make_async_copy(
            cb_hbm.at[pl.ds(pl.multiple_of(me_i * 32 + n * 16, 16), 16), :],
            cbf.at[me_z, x, y, core, n], in_sem.at[chunks + 1 + n],
        )
        for n in range(2)
    ]
    for copy in own:
        copy.start()
    load_cb = pltpu.make_async_copy(cb_hbm, cb, in_sem.at[chunks])
    load_cb.start()

    barrier = pltpu.get_barrier_semaphore()

    def greet_items(k, carry):
        pl.semaphore_signal(
            barrier, inc=1, device_id={"items": lax.rem(me_i + k, items_n)}, device_id_type=MESH
        )
        return carry

    def greet_codes(k, carry):
        pl.semaphore_signal(
            barrier, inc=1, device_id={"codes": lax.rem(me_z + k, codes_n)}, device_id_type=MESH
        )
        return carry

    lax.fori_loop(1, codes_n, greet_codes, 0)
    lax.fori_loop(1, items_n, greet_items, 0)

    pl.semaphore_wait(barrier, items_n + codes_n - 2)

    def hop(direction, h, u):
        z = me_z - (h - 1) if direction == 0 else me_z + (h - 1)
        z = lax.rem(z + codes_n, codes_n)
        ref = cbf.at[z, x, y, core] if u == 0 else block(u - 1, z)
        return remote(
            ref, ref, ring_send.at[direction, h - 1, u], ring_recv.at[direction, h - 1, u],
            {"codes": right if direction == 0 else left},
        )

    for copy in own:
        copy.wait()
    for u in range(chunks + 1):
        for d in range(2):
            hop(d, 1, u).start()
    load_cb.wait()
    wide = cb[...].astype(jnp.float32)
    inv_col[...] = jnp.broadcast_to(
        lax.rsqrt(jnp.mean(wide * wide, axis=1, keepdims=True) + EPS), inv_col.shape
    )
    for b in range(codes // LANES):
        tsend[b:b + 1, :] = jnp.transpose(inv_col[b * LANES:(b + 1) * LANES, :])[0:1, :]
    cinv[me_z] = tsend[...]

    def plane_copies(part):
        if part == 0:
            a, b = cbf.at[:, x, y, core, 0], cbf.at[:, x, y, core, 1]
        else:
            zs = pl.ds((part - 1) * (codes_n // PARTS), codes_n // PARTS)
            b, a = cbf.at[zs, :, y, core, 0], cbf.at[zs, x, :, core, 1]
        out = []
        for k in range(1, SIDE):
            to_x = at_plane(lax.rem(x + k, SIDE), y, core)
            to_y = at_plane(x, lax.rem(y + k, SIDE), core)
            out.append(remote(a, a, plane_send.at[part, 0], plane_recv.at[part, 0], to_x))
            out.append(remote(b, b, plane_send.at[part, 1], plane_recv.at[part, 1], to_y))
        return out

    def plane_start(part):
        for copy in plane_copies(part):
            copy.start()

    def plane_wait(part, sem):
        for way in range(2):
            if part == 0:
                ref = cbf.at[:, 0, pl.ds(0, SIDE - 1), 0, 0]
            else:
                ref = cbf.at[pl.ds(0, codes_n // PARTS), :, pl.ds(0, SIDE - 1), 0, 0]
            wait_bytes(ref, sem.at[part, way])

    def pair_copy(part):
        ref = cbf.at[pl.ds(part * (codes_n // PARTS), codes_n // PARTS), :, :, core]
        return remote(ref, ref, pair_send.at[part], pair_recv.at[part], at_plane(x, y, 1 - core))

    def tile(c):
        r_wide = R[c].astype(jnp.float32)
        inv_row[...] = lax.rsqrt(
            jnp.mean(r_wide * r_wide, axis=0, keepdims=True) + EPS
        ) * (SMOOTHING * LOG2E / F)

        def tile_step(m, carry):
            at = pl.ds(pl.multiple_of(m * TILE, TILE), TILE)
            dots = jnp.dot(cb[at, :], R[c], preferred_element_type=jnp.float32)
            scale = inv_col[at, :]
            values = []
            for q in range(CHUNK // LANES):
                lanes = slice(q * LANES, (q + 1) * LANES)
                value = jnp.exp2(dots[:, lanes] * inv_row[:, lanes] * scale)
                K[at, c * CHUNK + q * LANES:c * CHUNK + (q + 1) * LANES] = value
                values.append(value)
            total = tree_sum(values)
            if c in first_tile:
                tacc[at, :] = total
            else:
                tacc[at, :] += total
            return carry

        lax.fori_loop(0, codes // TILE, tile_step, 0, unroll=True)

    plan = ring_plan(codes_n, chunks + 1)
    left_over = [sum(1 for d, h, u, then in plan if u == v) for v in range(chunks + 1)]
    first_tile = []
    for d, h, u, then in plan:
        hop(d, h, u).wait_recv()
        if then:
            hop(d, h + 1, u).start()
        left_over[u] -= 1
        if left_over[u] == 0:
            if u == 0:
                plane_start(0)
            else:
                if not first_tile:
                    first_tile.append(u - 1)
                else:
                    first_tile[:] = [-1]
                tile(u - 1)

    groups = codes // 8
    lane_chunks = rows // LANES

    ring_order = sorted(range(1, codes_n), key=lambda k: -min(k, codes_n - k))
    plane_order = sorted(
        [(dx, dy, dc) for dx in range(SIDE) for dy in range(SIDE) for dc in range(2)],
        key=lambda o: -(min(o[0], SIDE - o[0]) + min(o[1], SIDE - o[1])),
    )

    def exchange_codes(ref, send_sem, recv_sem):
        for k in ring_order:
            to = {"codes": lax.rem(me_z + k, codes_n)}
            remote(ref, ref, send_sem, recv_sem, to).start()

    def exchange_items(ref, send_sem, recv_sem):
        for dx, dy, dc in plane_order:
            if dx or dy or dc:
                to = at_plane(lax.rem(x + dx, SIDE), lax.rem(y + dy, SIDE), lax.rem(core + dc, 2))
                remote(ref, ref, send_sem, recv_sem, to).start()

    def all_but_one(buf, count, sem):
        wait_bytes(buf.at[pl.ds(0, count - 1)], sem)

    def second_rows():
        rows2[...] = jnp.transpose(R[me_z])
        wide2 = rows2[...].astype(jnp.float32)
        a2[...] = jnp.broadcast_to(
            lax.rsqrt(jnp.mean(wide2 * wide2, axis=1, keepdims=True) + EPS)
            * (SMOOTHING * LOG2E / F), a2.shape)

    def second_tile(part):
        def step(n, carry):
            z, k = n // 4, lax.rem(n, 4)
            some = cbf[z, k].reshape(codes // 4, F)
            dots = lax.dot_general(
                rows2[...], some, (((1,), (1,)), ((), ())), preferred_element_type=jnp.float32
            )
            for q in range(2):
                scale = cinv[z, pl.ds(2 * k + q, 1), :]
                value = jnp.exp2(dots[:, q * LANES:(q + 1) * LANES] * a2[...] * scale)
                K2[:, pl.ds(pl.multiple_of(n * 256 + q * LANES, LANES), LANES)] = value
            return carry

        steps = 4 * codes_n // PARTS
        lax.fori_loop(part * steps, (part + 1) * steps, step, 0, unroll=4)

    def send_inv(k, carry):
        remote(cinv.at[me_z], cinv.at[me_z], z_send, z_recv,
               {"codes": lax.rem(me_z + k, codes_n)}).start()
        return carry

    lax.fori_loop(1, codes_n, send_inv, 0)

    for it in range(ITERS):
        last = it == ITERS - 1
        if it > 0:
            s_bcast = [
                jnp.broadcast_to(s_ref[q:q + 1, :], (8, LANES)) for q in range(lane_chunks)
            ]

            def col_step(g, carry):
                at = pl.ds(pl.multiple_of(g * 8, 8), 8)
                tacc[at, :] = tree_sum([
                    K[at, q * LANES:(q + 1) * LANES] * s_bcast[q] for q in range(lane_chunks)
                ])
                return carry

            lax.fori_loop(0, groups, col_step, 0, unroll=4)
        for b in range(codes // LANES):
            blockT = jnp.transpose(tacc[b * LANES:(b + 1) * LANES, :])
            tsend[b:b + 1, :] = jnp.sum(blockT, axis=0, keepdims=True)
        colbuf[it, me_i] = tsend[...]
        exchange_items(colbuf.at[it, me_i], col_send.at[it], col_recv.at[it])
        if it == 0:
            for d, h, u, then in plan:
                hop(d, h, u).wait_send()
            second_rows()
            plane_wait(0, plane_recv)
        if it == 1:
            for part in (0, 1):
                plane_wait(1 + part, plane_recv)
                pair_copy(part).start()
            plane_wait(0, plane_send)
            all_but_one(colbuf.at[0], items_n, col_send.at[0])
            all_but_one(rowbuf.at[0], codes_n, row_send.at[0])
            all_but_one(cinv, codes_n, z_recv)
            all_but_one(cinv, codes_n, z_send)
        if last:
            for part in (2, 3):
                plane_wait(1 + part, plane_recv)
                pair_copy(part).start()
            for part in (2, 3):
                pair_copy(part).wait_recv()
                second_tile(part)
        all_but_one(colbuf.at[it], items_n, col_recv.at[it])
        if not last:
            plane_start(1 + 2 * it)
            plane_start(2 + 2 * it)
        w = total_items / jnp.sum(colbuf[it], axis=0)
        if last:
            w_out = w * math.exp(SHIFT)
            for b in range(codes // LANES):
                out_ref[feats + 1:feats + 2, b * LANES:(b + 1) * LANES] = w_out[b:b + 1, :]
            wbuf[me_z] = w * (1.0 / total_codes)
            for k in ring_order:
                remote(wbuf.at[me_z], wbuf.at[me_z], w_send, w_recv.at[k],
                       {"codes": lax.rem(me_z + k, codes_n)}).start()
            for past in (1, 2):
                all_but_one(colbuf.at[past], items_n, col_send.at[past])
            all_but_one(rowbuf.at[1], codes_n, row_send.at[1])
            for part in range(PARTS):
                plane_wait(1 + part, plane_send)
                pair_copy(part).wait_send()
            break
        for b in range(codes // LANES):
            W[b * LANES:(b + 1) * LANES, :] = jnp.transpose(
                jnp.broadcast_to(w[b:b + 1, :], (LANES, LANES))
            )

        def row_step(g, acc):
            at = pl.ds(pl.multiple_of(g * 8, 8), 8)
            weight = W[at, :]
            return tuple(
                acc[q] + K[at, q * LANES:(q + 1) * LANES] * weight for q in range(lane_chunks)
            )

        acc = lax.fori_loop(
            0, groups, row_step,
            tuple(jnp.zeros((8, LANES), jnp.float32) for _ in range(lane_chunks)), unroll=4,
        )
        for q in range(lane_chunks):
            s_ref[q:q + 1, :] = jnp.sum(acc[q], axis=0, keepdims=True)
        rowbuf[it, me_z] = s_ref[...]
        exchange_codes(rowbuf.at[it, me_z], row_send.at[it], row_recv.at[it])
        if it == 1:
            for part in (0, 1):
                pair_copy(part).wait_recv()
                second_tile(part)
        all_but_one(rowbuf.at[it], codes_n, row_recv.at[it])
        s_ref[...] = total_codes / jnp.sum(rowbuf[it], axis=0)

    def part_of(z):
        return pl.ds(pl.multiple_of(z * feats, feats), feats)

    def shares_of(z, at, first, out):
        total = []
        for q in range(codes // LANES):
            lanes = slice(z * codes + q * LANES, z * codes + (q + 1) * LANES)
            value = K2[at, lanes] * wbuf[z, q:q + 1, :]
            total.append(value)
            out[:, q * LANES:(q + 1) * LANES] = value.astype(jnp.bfloat16)
        r2[...] = tree_sum(total) if first else r2[...] + tree_sum(total)

    def mix_of(z, first, src):
        some = jnp.dot(src[...], cbf[z].reshape(codes, F), preferred_element_type=jnp.float32)
        mix[...] = some if first else mix[...] + some

    def encode(b, values):
        near = values.astype(jnp.bfloat16)
        wide = near.astype(jnp.float32)
        left = (values - wide) * (LEVELS * 256.0 / jnp.maximum(jnp.abs(wide), 1e-30))
        left = jnp.clip(jnp.round(left), -LEVELS, LEVELS).reshape(codes_n, 2, feats // 2, LANES)
        softT[b, :, :feats, :] = near.reshape(codes_n, feats, LANES)
        softT[b, :, feats:, :] = (left[:, 0] * 16.0 + left[:, 1]).astype(jnp.bfloat16)

    def decode(coded):
        wide = coded[:feats, :].astype(jnp.float32)
        both = coded[feats:, :].astype(jnp.float32)
        high = jnp.round(both * (1.0 / 16.0))
        left = jnp.concatenate([high, both - 16.0 * high], axis=0)
        return wide + jnp.abs(wide) * (left * (1.0 / (LEVELS * 256.0)))

    for k in ring_order:
        wait_bytes(wbuf.at[0], w_recv.at[k])
    buffers = (shares_a, shares_b)

    def half_step(b, carry):
        at = pl.ds(pl.multiple_of(b * LANES, LANES), LANES)
        for z in range(codes_n):
            shares_of(z, at, z == 0, buffers[z % 2])
            if z > 0:
                mix_of(z - 1, z == 1, buffers[(z - 1) % 2])
        mix_of(codes_n - 1, False, buffers[(codes_n - 1) % 2])
        scale = 1.0 / jnp.sum(jnp.transpose(r2[...]), axis=0, keepdims=True)
        sbuf[me_z, pl.ds(b, 1), :] = scale
        encode(b, jnp.transpose(mix[...]))
        for k in ring_order:
            z = lax.rem(me_z + k, codes_n)
            remote(softT.at[b, z], land.at[b, me_z], out_send.at[b], out_recv.at[b],
                   {"codes": z}).start()
        land[b, me_z] = softT[b, me_z]
        return carry

    lax.fori_loop(0, mine // LANES, half_step, 0)
    exchange_codes(sbuf.at[me_z], out_send.at[2], out_recv.at[2])
    all_but_one(wbuf, codes_n, w_send)

    all_but_one(sbuf, codes_n, out_recv.at[2])
    for z in range(codes_n):
        for b in range(mine // LANES):
            n = z * (mine // LANES) + b
            out_ref[feats:feats + 1, n * LANES:(n + 1) * LANES] = sbuf[z, b:b + 1, :]
    for b in range(mine // LANES):
        all_but_one(land.at[b], codes_n, out_recv.at[b])
        for z in range(codes_n):
            n = z * (mine // LANES) + b
            out_ref[:feats, n * LANES:(n + 1) * LANES] = decode(land[b, z])
    for b in range(mine // LANES):
        all_but_one(land.at[b], codes_n, out_send.at[b])
    all_but_one(sbuf, codes_n, out_send.at[2])


def shards(residuals, codebook):
    items_n, codes_n = lax.axis_size("items"), lax.axis_size("codes")
    rows, feats = residuals.shape
    codes = codebook.shape[0]
    chunks = rows // CHUNK
    half = codes_n // 2
    mine = rows // codes_n
    f32, bf16 = jnp.float32, jnp.bfloat16
    hbm = pl.BlockSpec(memory_space=pltpu.HBM)
    vmem = pl.BlockSpec(memory_space=pltpu.VMEM)
    dma = pltpu.SemaphoreType.DMA
    out = pl.pallas_call(
        functools.partial(
            kernel, items_n, codes_n, float(rows * items_n), float(codes * codes_n)
        ),
        out_shape=jax.ShapeDtypeStruct((feats + 8, rows), f32),
        in_specs=[hbm, hbm],
        out_specs=vmem,
        scratch_shapes=[
            pltpu.VMEM((rows // LANES, LANES), f32),
            pltpu.VMEM((codes, F), bf16),
            pltpu.VMEM((codes_n, SIDE, SIDE, 2, 2, 16, F), bf16),
            pltpu.VMEM((chunks, F, CHUNK), bf16),
            pltpu.VMEM((codes, rows), f32),
            pltpu.VMEM((mine, codes * codes_n), f32),
            pltpu.VMEM((1, CHUNK), f32),
            pltpu.VMEM((codes, LANES), f32),
            pltpu.VMEM((codes, LANES), f32),
            pltpu.VMEM((codes, LANES), f32),
            pltpu.VMEM((codes // LANES, LANES), f32),
            pltpu.VMEM((codes_n, codes // LANES, LANES), f32),
            pltpu.VMEM((codes_n, codes // LANES, LANES), f32),
            pltpu.VMEM((ITERS, items_n, codes // LANES, LANES), f32),
            pltpu.VMEM((ITERS - 1, codes_n, rows // LANES, LANES), f32),
            pltpu.VMEM((codes_n, mine // LANES, LANES), f32),
            pltpu.VMEM((mine, F), bf16),
            pltpu.VMEM((mine, LANES), f32),
            pltpu.VMEM((LANES, LANES), f32),
            pltpu.VMEM((LANES, F), f32),
            pltpu.VMEM((LANES, codes), bf16),
            pltpu.VMEM((LANES, codes), bf16),
            pltpu.VMEM((mine // LANES, codes_n, feats + feats // 2, LANES), bf16),
            pltpu.VMEM((mine // LANES, codes_n, feats + feats // 2, LANES), bf16),
            dma((chunks + 3,)),
            dma((2, half, chunks + 1)),
            dma((2, half, chunks + 1)),
            dma((ITERS,)), dma((ITERS,)), dma((ITERS - 1,)), dma((ITERS - 1,)),
            dma, dma((codes_n,)),
            dma, dma,
            dma((PARTS + 1, 2)), dma((PARTS + 1, 2)),
            dma((PARTS,)), dma((PARTS,)),
            dma((3,)), dma((3,)),
        ],
        compiler_params=pltpu.CompilerParams(
            collective_id=0, has_side_effects=True, vmem_limit_bytes=VMEM_BYTES
        ),
    )(pltpu.with_memory_space_constraint(residuals.T, pltpu.HBM), pltpu.with_memory_space_constraint(codebook, pltpu.HBM))
    items_scale = out[feats]
    return (out[:feats] * items_scale[None, :]).T, items_scale, out[feats + 1, :codes]


def solution(mesh):
    placed = (P("items", "codes"), P("codes", None))
    return jax.shard_map(
        shards,
        mesh=mesh,
        in_specs=placed,
        out_specs=(P("items", "codes"), P("items"), P("codes")),
        check_vma=False,
    )
```

```python
import functools
import math

import jax
import jax.numpy as jnp
from jax import lax
from jax.experimental import pallas as pl
from jax.experimental.pallas import tpu as pltpu
from jax.sharding import PartitionSpec as P

F = 256
ITERS = 3
EPS = 1e-06
SMOOTHING = 32.0
SHIFT = 2.0
LOG2E = 1.4426950408889634

LANES = 128
CHUNK = 256
TILE = 256
PARTS = 4
LEVELS = 7.0
VMEM_BYTES = 48 * 1024 * 1024
SIDE = 4
MESH = pl.DeviceIdType.MESH


def ring_plan(codes_n, units):
    half = codes_n // 2

    def goes(d, h, u):
        return h < half or (h == half and (u % 2 == 0) == (d == 0))

    return [
        (d, h, u, goes(d, h + 1, u))
        for h in range(1, half + 1) for u in range(units) for d in range(2) if goes(d, h, u)
    ]


def tree_sum(terms):
    while len(terms) > 1:
        terms = [a + b for a, b in zip(terms[::2], terms[1::2])] + terms[len(terms) // 2 * 2:]
    return terms[0]


def kernel(
    items_n, codes_n, total_items, total_codes,
    rt_hbm, cb_hbm, soft_ref, s_ref, w_ref,
    cb, cbf, R, K, K2, inv_row, inv_col, tacc, W, tsend, cinv, wbuf, colbuf, rowbuf, sbuf,
    rows2, a2, r2, mix, shares_a, shares_b, softT, land,
    in_sem, ring_send, ring_recv, col_send, col_recv, row_send, row_recv,
    w_send, w_recv, z_send, z_recv, plane_send, plane_recv, pair_send, pair_recv, out_send, out_recv,
):
    me_i = lax.axis_index("items")
    me_z = lax.axis_index("codes")
    x, y, core = me_i // (2 * SIDE), lax.rem(me_i // 2, SIDE), lax.rem(me_i, 2)
    rows = rt_hbm.shape[1]
    codes = cb_hbm.shape[0]
    feats = rt_hbm.shape[0]
    chunks = rows // CHUNK
    mine = rows // codes_n
    right = lax.rem(me_z + 1, codes_n)
    left = lax.rem(me_z + codes_n - 1, codes_n)
    half = codes_n // 2

    def remote(src, dst, send, recv, device):
        return pltpu.make_async_remote_copy(
            src_ref=src, dst_ref=dst, send_sem=send, recv_sem=recv,
            device_id=device, device_id_type=MESH,
        )

    def wait_bytes(ref, sem):
        pltpu.make_async_copy(ref, ref, sem).wait()

    def at_plane(px, py, pcore):
        return {"items": (px * SIDE + py) * 2 + pcore}

    def block(c, z):
        return R.at[c, pl.ds(pl.multiple_of(z * feats, feats), feats), :]

    own = [
        pltpu.make_async_copy(
            rt_hbm.at[:, c * CHUNK:(c + 1) * CHUNK], block(c, me_z), in_sem.at[c]
        )
        for c in range(chunks)
    ]
    own += [
        pltpu.make_async_copy(
            cb_hbm.at[pl.ds(pl.multiple_of(me_i * 32 + n * 16, 16), 16), :],
            cbf.at[me_z, x, y, core, n], in_sem.at[chunks + 1 + n],
        )
        for n in range(2)
    ]
    for copy in own:
        copy.start()
    load_cb = pltpu.make_async_copy(cb_hbm, cb, in_sem.at[chunks])
    load_cb.start()

    barrier = pltpu.get_barrier_semaphore()

    def greet_items(k, carry):
        pl.semaphore_signal(
            barrier, inc=1, device_id={"items": lax.rem(me_i + k, items_n)}, device_id_type=MESH
        )
        return carry

    def greet_codes(k, carry):
        pl.semaphore_signal(
            barrier, inc=1, device_id={"codes": lax.rem(me_z + k, codes_n)}, device_id_type=MESH
        )
        return carry

    lax.fori_loop(1, codes_n, greet_codes, 0)
    lax.fori_loop(1, items_n, greet_items, 0)

    pl.semaphore_wait(barrier, items_n + codes_n - 2)

    def hop(direction, h, u):
        z = me_z - (h - 1) if direction == 0 else me_z + (h - 1)
        z = lax.rem(z + codes_n, codes_n)
        ref = cbf.at[z, x, y, core] if u == 0 else block(u - 1, z)
        return remote(
            ref, ref, ring_send.at[direction, h - 1, u], ring_recv.at[direction, h - 1, u],
            {"codes": right if direction == 0 else left},
        )

    for copy in own:
        copy.wait()
    for u in range(chunks + 1):
        for d in range(2):
            hop(d, 1, u).start()
    load_cb.wait()
    wide = cb[...].astype(jnp.float32)
    inv_col[...] = jnp.broadcast_to(
        lax.rsqrt(jnp.mean(wide * wide, axis=1, keepdims=True) + EPS), inv_col.shape
    )
    for b in range(codes // LANES):
        tsend[b:b + 1, :] = jnp.transpose(inv_col[b * LANES:(b + 1) * LANES, :])[0:1, :]
    cinv[me_z] = tsend[...]

    def plane_copies(part):
        if part == 0:
            a, b = cbf.at[:, x, y, core, 0], cbf.at[:, x, y, core, 1]
        else:
            zs = pl.ds((part - 1) * (codes_n // PARTS), codes_n // PARTS)
            b, a = cbf.at[zs, :, y, core, 0], cbf.at[zs, x, :, core, 1]
        out = []
        for k in range(1, SIDE):
            to_x = at_plane(lax.rem(x + k, SIDE), y, core)
            to_y = at_plane(x, lax.rem(y + k, SIDE), core)
            out.append(remote(a, a, plane_send.at[part, 0], plane_recv.at[part, 0], to_x))
            out.append(remote(b, b, plane_send.at[part, 1], plane_recv.at[part, 1], to_y))
        return out

    def plane_start(part):
        for copy in plane_copies(part):
            copy.start()

    def plane_wait(part, sem):
        for way in range(2):
            if part == 0:
                ref = cbf.at[:, 0, pl.ds(0, SIDE - 1), 0, 0]
            else:
                ref = cbf.at[pl.ds(0, codes_n // PARTS), :, pl.ds(0, SIDE - 1), 0, 0]
            wait_bytes(ref, sem.at[part, way])

    def pair_copy(part):
        ref = cbf.at[pl.ds(part * (codes_n // PARTS), codes_n // PARTS), :, :, core]
        return remote(ref, ref, pair_send.at[part], pair_recv.at[part], at_plane(x, y, 1 - core))

    def tile(c):
        r_wide = R[c].astype(jnp.float32)
        inv_row[...] = lax.rsqrt(
            jnp.mean(r_wide * r_wide, axis=0, keepdims=True) + EPS
        ) * (SMOOTHING * LOG2E / F)

        def tile_step(m, carry):
            at = pl.ds(pl.multiple_of(m * TILE, TILE), TILE)
            dots = jnp.dot(cb[at, :], R[c], preferred_element_type=jnp.float32)
            scale = inv_col[at, :]
            values = []
            for q in range(CHUNK // LANES):
                lanes = slice(q * LANES, (q + 1) * LANES)
                value = jnp.exp2(dots[:, lanes] * inv_row[:, lanes] * scale)
                K[at, c * CHUNK + q * LANES:c * CHUNK + (q + 1) * LANES] = value
                values.append(value)
            total = tree_sum(values)
            if c in first_tile:
                tacc[at, :] = total
            else:
                tacc[at, :] += total
            return carry

        lax.fori_loop(0, codes // TILE, tile_step, 0, unroll=True)

    plan = ring_plan(codes_n, chunks + 1)
    left_over = [sum(1 for d, h, u, then in plan if u == v) for v in range(chunks + 1)]
    first_tile = []
    for d, h, u, then in plan:
        hop(d, h, u).wait_recv()
        if then:
            hop(d, h + 1, u).start()
        left_over[u] -= 1
        if left_over[u] == 0:
            if u == 0:
                plane_start(0)
            else:
                if not first_tile:
                    first_tile.append(u - 1)
                else:
                    first_tile[:] = [-1]
                tile(u - 1)

    groups = codes // 8
    lane_chunks = rows // LANES

    ring_order = sorted(range(1, codes_n), key=lambda k: -min(k, codes_n - k))
    plane_order = sorted(
        [(dx, dy, dc) for dx in range(SIDE) for dy in range(SIDE) for dc in range(2)],
        key=lambda o: -(min(o[0], SIDE - o[0]) + min(o[1], SIDE - o[1])),
    )

    def exchange_codes(ref, send_sem, recv_sem):
        for k in ring_order:
            to = {"codes": lax.rem(me_z + k, codes_n)}
            remote(ref, ref, send_sem, recv_sem, to).start()

    def exchange_items(ref, send_sem, recv_sem):
        for dx, dy, dc in plane_order:
            if dx or dy or dc:
                to = at_plane(lax.rem(x + dx, SIDE), lax.rem(y + dy, SIDE), lax.rem(core + dc, 2))
                remote(ref, ref, send_sem, recv_sem, to).start()

    def all_but_one(buf, count, sem):
        wait_bytes(buf.at[pl.ds(0, count - 1)], sem)

    def second_rows():
        rows2[...] = jnp.transpose(R[me_z])
        wide2 = rows2[...].astype(jnp.float32)
        a2[...] = jnp.broadcast_to(
            lax.rsqrt(jnp.mean(wide2 * wide2, axis=1, keepdims=True) + EPS)
            * (SMOOTHING * LOG2E / F), a2.shape)

    def second_tile(part):
        def step(n, carry):
            z, k = n // 4, lax.rem(n, 4)
            some = cbf[z, k].reshape(codes // 4, F)
            dots = lax.dot_general(
                rows2[...], some, (((1,), (1,)), ((), ())), preferred_element_type=jnp.float32
            )
            for q in range(2):
                scale = cinv[z, pl.ds(2 * k + q, 1), :]
                value = jnp.exp2(dots[:, q * LANES:(q + 1) * LANES] * a2[...] * scale)
                K2[:, pl.ds(pl.multiple_of(n * 256 + q * LANES, LANES), LANES)] = value
            return carry

        steps = 4 * codes_n // PARTS
        lax.fori_loop(part * steps, (part + 1) * steps, step, 0, unroll=4)

    def send_inv(k, carry):
        remote(cinv.at[me_z], cinv.at[me_z], z_send, z_recv,
               {"codes": lax.rem(me_z + k, codes_n)}).start()
        return carry

    lax.fori_loop(1, codes_n, send_inv, 0)

    for it in range(ITERS):
        last = it == ITERS - 1
        if it > 0:
            s_bcast = [
                jnp.broadcast_to(s_ref[q:q + 1, :], (8, LANES)) for q in range(lane_chunks)
            ]

            def col_step(g, carry):
                at = pl.ds(pl.multiple_of(g * 8, 8), 8)
                tacc[at, :] = tree_sum([
                    K[at, q * LANES:(q + 1) * LANES] * s_bcast[q] for q in range(lane_chunks)
                ])
                return carry

            lax.fori_loop(0, groups, col_step, 0, unroll=4)
        for b in range(codes // LANES):
            blockT = jnp.transpose(tacc[b * LANES:(b + 1) * LANES, :])
            tsend[b:b + 1, :] = jnp.sum(blockT, axis=0, keepdims=True)
        colbuf[it, me_i] = tsend[...]
        exchange_items(colbuf.at[it, me_i], col_send.at[it], col_recv.at[it])
        if it == 0:
            for d, h, u, then in plan:
                hop(d, h, u).wait_send()
            second_rows()
            plane_wait(0, plane_recv)
        if it == 1:
            for part in (0, 1):
                plane_wait(1 + part, plane_recv)
                pair_copy(part).start()
            plane_wait(0, plane_send)
            all_but_one(colbuf.at[0], items_n, col_send.at[0])
            for side in range(2):
                all_but_one(rowbuf.at[0, side], codes_n, row_send.at[0, side])
            all_but_one(cinv, codes_n, z_recv)
            all_but_one(cinv, codes_n, z_send)
        if last:
            for part in (2, 3):
                plane_wait(1 + part, plane_recv)
                pair_copy(part).start()
            for part in (2, 3):
                pair_copy(part).wait_recv()
                second_tile(part)
        all_but_one(colbuf.at[it], items_n, col_recv.at[it])
        if not last:
            plane_start(1 + 2 * it)
            plane_start(2 + 2 * it)
        w = total_items / jnp.sum(colbuf[it], axis=0)
        if last:
            w_ref[...] = w * math.exp(SHIFT)
            wbuf[me_z] = w * (1.0 / total_codes)
            for k in ring_order:
                remote(wbuf.at[me_z], wbuf.at[me_z], w_send, w_recv.at[k],
                       {"codes": lax.rem(me_z + k, codes_n)}).start()
            for past in (1, 2):
                all_but_one(colbuf.at[past], items_n, col_send.at[past])
            for side in range(2):
                all_but_one(rowbuf.at[1, side], codes_n, row_send.at[1, side])
            for part in range(PARTS):
                plane_wait(1 + part, plane_send)
                pair_copy(part).wait_send()
            break
        for b in range(codes // LANES):
            W[b * LANES:(b + 1) * LANES, :] = jnp.transpose(
                jnp.broadcast_to(w[b:b + 1, :], (LANES, LANES))
            )

        width = lane_chunks // 2
        for side in range(2):
            def row_step(g, acc, side=side):
                at = pl.ds(pl.multiple_of(g * 8, 8), 8)
                weight = W[at, :]
                return tuple(
                    acc[q] + K[at, (side * width + q) * LANES:(side * width + q + 1) * LANES] * weight
                    for q in range(width)
                )

            acc = lax.fori_loop(
                0, groups, row_step,
                tuple(jnp.zeros((8, LANES), jnp.float32) for _ in range(width)), unroll=8,
            )
            for q in range(width):
                rowbuf[it, side, me_z, q:q + 1, :] = jnp.sum(acc[q], axis=0, keepdims=True)
            exchange_codes(
                rowbuf.at[it, side, me_z], row_send.at[it, side], row_recv.at[it, side]
            )
        if it == 1:
            for part in (0, 1):
                pair_copy(part).wait_recv()
                second_tile(part)
        for side in range(2):
            all_but_one(rowbuf.at[it, side], codes_n, row_recv.at[it, side])
            at = slice(side * width, (side + 1) * width)
            s_ref[at, :] = total_codes / jnp.sum(rowbuf[it, side], axis=0)

    def part_of(z):
        return pl.ds(pl.multiple_of(z * feats, feats), feats)

    def shares_of(z, at, first, out):
        total = []
        for q in range(codes // LANES):
            lanes = slice(z * codes + q * LANES, z * codes + (q + 1) * LANES)
            value = K2[at, lanes] * wbuf[z, q:q + 1, :]
            total.append(value)
            out[:, q * LANES:(q + 1) * LANES] = value.astype(jnp.bfloat16)
        r2[...] = tree_sum(total) if first else r2[...] + tree_sum(total)

    def mix_of(z, first, src):
        some = jnp.dot(src[...], cbf[z].reshape(codes, F), preferred_element_type=jnp.float32)
        mix[...] = some if first else mix[...] + some

    def encode(b, values):
        near = values.astype(jnp.bfloat16)
        wide = near.astype(jnp.float32)
        left = (values - wide) * (LEVELS * 256.0 / jnp.maximum(jnp.abs(wide), 1e-30))
        left = jnp.clip(jnp.round(left), -LEVELS, LEVELS).reshape(codes_n, 2, feats // 2, LANES)
        softT[b, :, :feats, :] = near.reshape(codes_n, feats, LANES)
        softT[b, :, feats:, :] = (left[:, 0] * 16.0 + left[:, 1]).astype(jnp.bfloat16)

    def decode(coded):
        wide = coded[:feats, :].astype(jnp.float32)
        both = coded[feats:, :].astype(jnp.float32)
        high = jnp.round(both * (1.0 / 16.0))
        left = jnp.concatenate([high, both - 16.0 * high], axis=0)
        return wide + jnp.abs(wide) * (left * (1.0 / (LEVELS * 256.0)))

    for k in ring_order:
        wait_bytes(wbuf.at[0], w_recv.at[k])
    buffers = (shares_a, shares_b)

    def half_step(b, carry):
        at = pl.ds(pl.multiple_of(b * LANES, LANES), LANES)
        for z in range(codes_n):
            shares_of(z, at, z == 0, buffers[z % 2])
            if z > 0:
                mix_of(z - 1, z == 1, buffers[(z - 1) % 2])
        mix_of(codes_n - 1, False, buffers[(codes_n - 1) % 2])
        scale = 1.0 / jnp.sum(jnp.transpose(r2[...]), axis=0, keepdims=True)
        sbuf[me_z, pl.ds(b, 1), :] = scale
        encode(b, jnp.transpose(mix[...]) * scale)
        for k in ring_order:
            z = lax.rem(me_z + k, codes_n)
            remote(softT.at[b, z], land.at[b, me_z], out_send.at[b], out_recv.at[b],
                   {"codes": z}).start()
        land[b, me_z] = softT[b, me_z]
        return carry

    lax.fori_loop(0, mine // LANES, half_step, 0)
    exchange_codes(sbuf.at[me_z], out_send.at[2], out_recv.at[2])
    all_but_one(wbuf, codes_n, w_send)

    all_but_one(sbuf, codes_n, out_recv.at[2])
    for z in range(codes_n):
        for b in range(mine // LANES):
            n = z * (mine // LANES) + b
            s_ref[n:n + 1, :] = sbuf[z, b:b + 1, :]
    for b in range(mine // LANES):
        all_but_one(land.at[b], codes_n, out_recv.at[b])
        for z in range(codes_n):
            n = z * (mine // LANES) + b
            soft_ref[:, n * LANES:(n + 1) * LANES] = decode(land[b, z])
    for b in range(mine // LANES):
        all_but_one(land.at[b], codes_n, out_send.at[b])
    all_but_one(sbuf, codes_n, out_send.at[2])


def shards(residuals, codebook):
    items_n, codes_n = lax.axis_size("items"), lax.axis_size("codes")
    rows, feats = residuals.shape
    codes = codebook.shape[0]
    chunks = rows // CHUNK
    half = codes_n // 2
    mine = rows // codes_n
    f32, bf16 = jnp.float32, jnp.bfloat16
    hbm = pl.BlockSpec(memory_space=pltpu.HBM)
    vmem = pl.BlockSpec(memory_space=pltpu.VMEM)
    dma = pltpu.SemaphoreType.DMA
    softT, items_scale, code_weights = pl.pallas_call(
        functools.partial(
            kernel, items_n, codes_n, float(rows * items_n), float(codes * codes_n)
        ),
        out_shape=(
            jax.ShapeDtypeStruct((feats, rows), f32),
            jax.ShapeDtypeStruct((rows // LANES, LANES), f32),
            jax.ShapeDtypeStruct((codes // LANES, LANES), f32),
        ),
        in_specs=[hbm, hbm],
        out_specs=(vmem, vmem, vmem),
        scratch_shapes=[
            pltpu.VMEM((codes, F), bf16),
            pltpu.VMEM((codes_n, SIDE, SIDE, 2, 2, 16, F), bf16),
            pltpu.VMEM((chunks, F, CHUNK), bf16),
            pltpu.VMEM((codes, rows), f32),
            pltpu.VMEM((mine, codes * codes_n), f32),
            pltpu.VMEM((1, CHUNK), f32),
            pltpu.VMEM((codes, LANES), f32),
            pltpu.VMEM((codes, LANES), f32),
            pltpu.VMEM((codes, LANES), f32),
            pltpu.VMEM((codes // LANES, LANES), f32),
            pltpu.VMEM((codes_n, codes // LANES, LANES), f32),
            pltpu.VMEM((codes_n, codes // LANES, LANES), f32),
            pltpu.VMEM((ITERS, items_n, codes // LANES, LANES), f32),
            pltpu.VMEM((ITERS - 1, 2, codes_n, rows // LANES // 2, LANES), f32),
            pltpu.VMEM((codes_n, mine // LANES, LANES), f32),
            pltpu.VMEM((mine, F), bf16),
            pltpu.VMEM((mine, LANES), f32),
            pltpu.VMEM((LANES, LANES), f32),
            pltpu.VMEM((LANES, F), f32),
            pltpu.VMEM((LANES, codes), bf16),
            pltpu.VMEM((LANES, codes), bf16),
            pltpu.VMEM((mine // LANES, codes_n, feats + feats // 2, LANES), bf16),
            pltpu.VMEM((mine // LANES, codes_n, feats + feats // 2, LANES), bf16),
            dma((chunks + 3,)),
            dma((2, half, chunks + 1)),
            dma((2, half, chunks + 1)),
            dma((ITERS,)), dma((ITERS,)), dma((ITERS - 1, 2)), dma((ITERS - 1, 2)),
            dma, dma((codes_n,)),
            dma, dma,
            dma((PARTS + 1, 2)), dma((PARTS + 1, 2)),
            dma((PARTS,)), dma((PARTS,)),
            dma((3,)), dma((3,)),
        ],
        compiler_params=pltpu.CompilerParams(
            collective_id=0, has_side_effects=True, vmem_limit_bytes=VMEM_BYTES
        ),
    )(pltpu.with_memory_space_constraint(residuals.T, pltpu.HBM), pltpu.with_memory_space_constraint(codebook, pltpu.HBM))
    return softT.T, items_scale.reshape(rows), code_weights.reshape(codes)


def solution(mesh):
    placed = (P("items", "codes"), P("codes", None))
    return jax.shard_map(
        shards,
        mesh=mesh,
        in_specs=placed,
        out_specs=(P("items", "codes"), P("items"), P("codes")),
        check_vma=False,
    )
```
